128 devices in a mesh: row: 16 (over y, z), col: 8 (over x, core).
Axes of the slice: x: 4, y: 4, z: 4, core: 2. Of those that a mesh axis runs over, the one named last changes fastest.
Arguments:
- clips: bfloat16 [8192, 768], P('row', 'col'), may hold values from -512 to 512
- captions: bfloat16 [16384, 768], P('col', 'row'), may hold values from -32 to 32
- caption_owner: int32 [16384], P('col'), may hold values from 0 to 8191, as said below
Outputs:
- loss: float32 [], replicated
- clip_grad: float32 [8192, 768], P(('row', 'col'))
- caption_grad: float32 [16384, 768], P(('col', 'row'))
The draws below stay inside these ranges and needn't reach their ends.
Inputs may be any that keep to these rules, and one draw needn't show every extreme that they name: `caption_owner`: each clip index is named by exactly two captions.
All inputs are finite; a program needn't handle non-finite values.
Results may differ from the reference program's by a relative error of at most 0.00105.
The reference program's roundings to bfloat16 on the way count: a program that leaves them out, or rounds other values in their place, can miss the bound.
Values may be sent and summed in bfloat16 or wider, within the bound.
No kernel may reach another device: no remote copies, remote signals or barrier semaphores. Data moves between devices by JAX's collectives and lax.ppermute only.
A program may use at most 64 MiB of HBM per device.

```python
import math
import jax
import jax.numpy as jnp
from jax import lax

D = 768
ROUNDS = 3
CLIPS = 8192
CAPTIONS = 16384


def embed_bases(key):
    subkeys = jax.random.split(key, 8)
    clip_noise = jax.random.truncated_normal(subkeys[0], -6.0, 6.0, (CLIPS, D), jnp.float32)
    caption_noise = jax.random.truncated_normal(subkeys[1], -6.0, 6.0, (CAPTIONS, D), jnp.float32)
    clip_level = jax.random.uniform(subkeys[2], (CLIPS, 1), jnp.float32)
    caption_level = jax.random.uniform(subkeys[3], (CAPTIONS, 1), jnp.float32)
    clip_common = jax.random.normal(subkeys[4], (1, D), jnp.float32)
    caption_common = jax.random.normal(subkeys[5], (1, D), jnp.float32)
    strength = jax.random.uniform(subkeys[6], (CLIPS // 2, 1), jnp.float32, 110.0, 280.0) / math.sqrt(D)
    copy_noise = jax.random.normal(subkeys[7], (CAPTIONS, D), jnp.float32)
    return (clip_noise, caption_noise, clip_level, caption_level, clip_common, caption_common, strength, copy_noise)


def caption_table(bases, lowest, highest):
    caption_noise = bases[1]
    caption_level = bases[3]
    copy_noise = bases[7]
    ratio = jnp.exp(math.log(lowest) + caption_level * (math.log(highest) - math.log(lowest)))
    table = 1.4 * ratio * caption_noise
    before = jnp.concatenate([table[:1], table[:-1]], axis=0)
    before_ratio = jnp.concatenate([ratio[:1], ratio[:-1]], axis=0)
    caption_ids = jnp.arange(CAPTIONS, dtype=jnp.int32)[:, None]
    chosen = (caption_ids % 128 == 1).astype(jnp.float32)
    target = before + 0.42 * before_ratio * copy_noise
    return (table + chosen * (target - table), ratio)


def clip_table(bases, lowest, highest):
    clip_noise = bases[0]
    clip_level = bases[2]
    strength = bases[6]
    caption_rows, caption_ratio = caption_table(bases, lowest, highest)
    ratio = jnp.exp(math.log(lowest) + clip_level * (math.log(highest) - math.log(lowest)))
    table = 1.4 * ratio * clip_noise
    target = caption_rows.reshape(CLIPS // 2, 4, D)[:, 0]
    target_ratio = caption_ratio.reshape(CLIPS // 2, 4, 1)[:, 0]
    scaled_target = jnp.repeat(target / (1.4 * target_ratio) ** 2, 2, axis=0)
    video_index_list = jnp.arange(CLIPS, dtype=jnp.int32)[:, None]
    parity = (video_index_list % 2).astype(jnp.float32)
    strength_rows = jnp.repeat(strength, 2, axis=0) + 0.05 * parity
    aligned_rows = strength_rows * scaled_target + 0.5 * parity * clip_noise
    chosen = (video_index_list % 64 < 2).astype(jnp.float32)
    return table + chosen * (aligned_rows - table)


def draw_clips(key, part):
    bases = embed_bases(key)
    table = clip_table(bases, 0.5, 1.6)
    return jnp.clip(table, -512.0, 512.0).astype(jnp.bfloat16)


def draw_captions(key, part):
    bases = embed_bases(key)
    table, ratio = caption_table(bases, 0.5, 1.6)
    return jnp.clip(table, -32.0, 32.0).astype(jnp.bfloat16)


def draw_caption_owner(key, part):
    key = jax.random.fold_in(key, 5)
    ordering = jax.random.permutation(key, CAPTIONS)
    return (ordering // 2).astype(jnp.int32)


def setup_inputs(seed: int = 0) -> dict:
    keys = jax.random.split(jax.random.key(seed), 4)
    return {
        "clips": draw_clips(jax.random.fold_in(keys[3], 71), 0),
        "captions": draw_captions(jax.random.fold_in(keys[3], 71), 0),
        "caption_owner": draw_caption_owner(jax.random.fold_in(keys[3], 71), 0),
    }


diagonal_increment = 4.0
midway_portion = math.log(0.5)

def horizontal_softmax_denominator(entries_array):
    highest = lax.optimization_barrier(jnp.max(entries_array, axis=1))
    return highest + jnp.log(lax.optimization_barrier(jnp.sum(jnp.exp(entries_array - highest[:, None]), axis=1)))

def vertical_potential_refresh(highest, totals, entries_array):
    larger = jnp.maximum(highest, lax.optimization_barrier(jnp.max(entries_array, axis=0)))
    totals = totals * jnp.exp(highest - larger) + lax.optimization_barrier(jnp.sum(jnp.exp(entries_array - larger[None, :]), axis=0))
    return (larger, totals)

def reference(clips, captions, caption_owner):
    block_rows = min(512, CLIPS)
    block_count = CLIPS // block_rows
    clip_blocks = clips.reshape(block_count, block_rows, D)
    offsets = (jnp.arange(block_count, dtype=jnp.int32) * block_rows).astype(jnp.int32)
    logit_scale = 1.0 / math.sqrt(D)

    def tilted_affinity(frame_segment_piece, displacement):
        cosine_affinity = jnp.dot(frame_segment_piece, captions.T, preferred_element_type=jnp.float32) * logit_scale
        video_index_list = (displacement + jnp.arange(block_rows, dtype=jnp.int32)).astype(jnp.int32)
        matched_pairs = (caption_owner[None, :] == video_index_list[:, None]).astype(jnp.float32)
        return (cosine_affinity, cosine_affinity + diagonal_increment * matched_pairs)

    def row_pass(vertical_dual_potential):

        def single(member):
            frame_segment_piece, displacement = member
            cosine_affinity, raised_affinity = tilted_affinity(frame_segment_piece, displacement)
            return (horizontal_softmax_denominator(raised_affinity + vertical_dual_potential[None, :]), horizontal_softmax_denominator(cosine_affinity))
        shifted, plain_lse = lax.map(single, (clip_blocks, offsets))
        return (shifted.reshape(CLIPS), plain_lse.reshape(CLIPS))

    def col_pass(horizontal_dual_potential):
        rotated_block_list = horizontal_dual_potential.reshape(block_count, block_rows)

        def advance(accumulating_state, member):
            frame_segment_piece, displacement, potential_piece = member
            cosine_affinity, raised_affinity = tilted_affinity(frame_segment_piece, displacement)
            translated_moments = vertical_potential_refresh(accumulating_state[0], accumulating_state[1], raised_affinity + potential_piece[:, None])
            plain_stats = vertical_potential_refresh(accumulating_state[2], accumulating_state[3], cosine_affinity)
            return ((translated_moments[0], translated_moments[1], plain_stats[0], plain_stats[1]), None)
        lowest = jnp.full((CAPTIONS,), -jnp.inf, dtype=jnp.float32)
        zeroed = jnp.zeros((CAPTIONS,), dtype=jnp.float32)
        accumulating_state, unused = lax.scan(advance, (lowest, zeroed, lowest, zeroed), (clip_blocks, offsets, rotated_block_list))
        return (accumulating_state[0] + jnp.log(accumulating_state[1]), accumulating_state[2] + jnp.log(accumulating_state[3]))
    vertical_dual_potential = jnp.zeros((CAPTIONS,), dtype=jnp.float32)
    horizontal_dual_potential = jnp.zeros((CLIPS,), dtype=jnp.float32)
    col_lse = jnp.zeros((CAPTIONS,), dtype=jnp.float32)
    for sweep_index in range(ROUNDS):
        horizontal_dual_potential = -row_pass(vertical_dual_potential)[0]
        shifted, col_lse = col_pass(horizontal_dual_potential)
        vertical_dual_potential = midway_portion - shifted
    horizontal_normalizer, row_lse = row_pass(vertical_dual_potential)

    def gradient_block(accumulating_state, member):
        caption_acc, loss_acc = accumulating_state
        frame_segment_piece, displacement, normalizer_piece, lse_block, potential_piece = member
        cosine_affinity, raised_affinity = tilted_affinity(frame_segment_piece, displacement)
        horizontal_marginal = jnp.exp(raised_affinity + vertical_dual_potential[None, :] - normalizer_piece[:, None])
        vertical_marginal = jnp.exp(raised_affinity + potential_piece[:, None] + (vertical_dual_potential - midway_portion)[None, :])
        loss_part = jnp.sum(horizontal_marginal * (lse_block[:, None] - cosine_affinity)) / (2.0 * CLIPS)
        loss_part = loss_part + jnp.sum(vertical_marginal * (col_lse[None, :] - cosine_affinity)) / (2.0 * CAPTIONS)
        slope_bfloat_copy = (jnp.exp(cosine_affinity - lse_block[:, None]) - horizontal_marginal + 0.5 * (jnp.exp(cosine_affinity - col_lse[None, :]) - vertical_marginal)).astype(jnp.bfloat16)
        clip_part = jnp.dot(slope_bfloat_copy, captions, preferred_element_type=jnp.float32)
        caption_acc = caption_acc + jnp.dot(slope_bfloat_copy.T, frame_segment_piece, preferred_element_type=jnp.float32)
        return ((caption_acc, loss_acc + loss_part), clip_part)
    start_state = (jnp.zeros((CAPTIONS, D), dtype=jnp.float32), jnp.zeros((), dtype=jnp.float32))
    members = (clip_blocks, offsets, horizontal_normalizer.reshape(block_count, block_rows), row_lse.reshape(block_count, block_rows), horizontal_dual_potential.reshape(block_count, block_rows))
    (caption_grad, loss), clip_parts = lax.scan(gradient_block, start_state, members)
    return (loss, clip_parts.reshape(CLIPS, D), caption_grad)
```

```python
import math

import jax
import jax.numpy as jnp
from jax import lax
from jax.experimental import pallas as pl
from jax.experimental.pallas import tpu as pltpu
from jax.sharding import PartitionSpec as P

BOOST = 4.0
HALF_LOG = math.log(0.5)
WIDTH = 768
ROWS = 512
COLS = 2048
LANES = 128
TILES = COLS // LANES
SIDE = 4
CLIP_PIECE = 96
CAPTION_PIECE = 48
EXTRA = 16
PACKED = WIDTH + EXTRA
AWAY = (0, 1, 3, 2)
F32 = jnp.float32
BF16 = jnp.bfloat16

VM = pl.BlockSpec(memory_space=pltpu.VMEM)
SM = pl.BlockSpec(memory_space=pltpu.SMEM)


def call(
    kernel, args, outs, name, scratch=(), smem=0, limit=8, flops=0, moved=0, exps=0, specs=None, grid=()
):
    return pl.pallas_call(
        kernel,
        grid=grid,
        out_shape=outs,
        in_specs=specs or [SM] * smem + [VM] * (len(args) - smem),
        out_specs=[VM] * len(outs),
        scratch_shapes=list(scratch),
        compiler_params=pltpu.CompilerParams(vmem_limit_bytes=limit * 2**20),
        cost_estimate=pl.CostEstimate(flops=flops, bytes_accessed=moved, transcendentals=exps),
        name=name,
    )(*args)


def shape(dims, kind=F32):
    return jax.ShapeDtypeStruct(dims, kind)


def row_shift(value, step_y, step_z):
    pairs = [
        (y * SIDE + z, ((y + step_y) % SIDE) * SIDE + (z + step_z) % SIDE)
        for y in range(SIDE)
        for z in range(SIDE)
    ]
    return lax.ppermute(value, "row", pairs)


def col_shift(value, step_x, flip):
    pairs = [
        (x * 2 + k, ((x + step_x) % SIDE) * 2 + (k ^ flip)) for x in range(SIDE) for k in range(2)
    ]
    return lax.ppermute(value, "col", pairs)


AWAY = (0, 1, 3, 2)


def col_all(copies):
    return lax.all_to_all(copies, "col", 0, 0, tiled=True)


def row_all(copies):
    return lax.all_to_all(copies, "row", 0, 0, tiled=True)


def swap(value, bits):
    return lax.ppermute(value, "col", [(c, c ^ bits) for c in range(8)])


def along_z(values):
    return [values[0]] + [row_shift(v, 0, d) for v, d in zip(values[1:], AWAY[1:])]


def along_y(values):
    return [values[0]] + [row_shift(v, d, 0) for v, d in zip(values[1:], AWAY[1:])]


def down(line):
    return jnp.transpose(jnp.broadcast_to(line, (LANES, line.shape[1])))


def along(block):
    return jnp.sum(jnp.transpose(block), axis=0, keepdims=True)


def copy_out(sums, value):
    for k in range(sums.shape[0]):
        sums[k] = value


def integers(packed):
    return packed.astype(jnp.int32).astype(F32)


def scale_of(steps):
    return jnp.exp2(steps * (1 / 64)) * (1 / 32000)


def steps_of(peak):
    return jnp.ceil(jnp.log2(jnp.maximum(peak, 1e-30)) * 64.0)


def halfwords(numbers):
    return jnp.round(numbers).astype(jnp.int32).astype(jnp.int16)


def widen(packed):
    rows = packed.shape[0] - EXTRA
    tail = integers(packed[rows:])
    share = (tail[2:3] + tail[3:4] * 2.0**-14) * scale_of(tail[1:2])
    return integers(packed[0:rows]) * scale_of(tail[0:1]), share


ZERO = 0.0


def narrow(value, share, out, start):
    rows, lanes = value.shape
    steps = steps_of(jnp.max(jnp.abs(value), axis=0, keepdims=True))
    out[start : start + rows] = halfwords(value * (1.0 / scale_of(steps)))
    share = share + jnp.zeros((1, lanes), F32)
    share_steps = steps_of(jnp.abs(share))
    scaled = share * (1.0 / scale_of(share_steps))
    high = jnp.round(scaled)
    low = (scaled - high) * 2.0**14
    row = lax.broadcasted_iota(jnp.int32, (EXTRA, lanes), 0)
    tail = jnp.where(
        row == 0, steps, jnp.where(row == 1, share_steps, jnp.where(row == 2, high, low))
    )
    out[start + rows : start + rows + EXTRA] = halfwords(tail)


def gathered(parts):
    total = parts[0]
    for k in range(1, parts.shape[0]):
        total += parts[k]
    return total


def joined(lses):
    peak = jnp.max(lses, axis=0, keepdims=True)
    return peak + jnp.log(jnp.sum(jnp.exp(lses - peak), axis=0, keepdims=True))


def tile(t):
    return slice(t * LANES, (t + 1) * LANES)


def row_chunks(step, body):
    def run(i, carry):
        body(pl.ds(pl.multiple_of(i * step, step), step))
        return carry

    lax.fori_loop(0, ROWS // step, run, 0)


def local_kernel(captions, clips, beside, captions_out, clips_out):
    captions_out[...] = captions[...]
    clips_out[0:CLIP_PIECE] = clips[...]
    clips_out[CLIP_PIECE:] = beside[...]


def join_kernel(*refs):
    parts, out = refs[:-1], refs[-1]
    for k, part in enumerate(parts):
        out[:, k * COLS : (k + 1) * COLS] = part[...]


def join(parts):
    dims = (CAPTION_PIECE, len(parts) * COLS)
    return call(join_kernel, parts, [shape(dims, BF16)], "join", moved=2**21)[0]


def pair_kernel(first, second, out):
    rows = first.shape[0]
    out[0:rows] = first[...]
    out[rows:] = second[...]


def pair(first, second):
    dims = (2 * first.shape[0], ROWS)
    return call(pair_kernel, [first, second], [shape(dims, BF16)], "pair", moved=2**20)[0]


def clips_kernel(place, here, there, clips, clips_t):
    x, core = place[2] // 2, place[2] % 2
    near = x + 1 - 2 * (x % 2)
    for k, part in enumerate((here, there)):
        for i, chip in enumerate((x, near, 3 - x, 3 - near)):
            rows = pl.ds(pl.multiple_of((2 * chip + (core + k) % 2) * CLIP_PIECE, 16), CLIP_PIECE)
            clips_t[rows, :] = part[i * CLIP_PIECE : (i + 1) * CLIP_PIECE]
    clips[...] = jnp.transpose(clips_t[...])


def logits_kernel(place, owner, clips, *refs):
    from_z, from_y, outs, (acc0, acc1, peaks) = refs[:4], refs[4:7], refs[7:11], refs[11:]
    captions, plain, raised, stats = outs
    y, z = place[0], place[1]

    def put(i, k, piece):
        block = ((y - AWAY[i] + SIDE) % SIDE) * SIDE + (z - AWAY[k] + SIDE) % SIDE
        rows = pl.ds(pl.multiple_of(block * CAPTION_PIECE, 16), CAPTION_PIECE)
        captions[rows, :] = piece

    for k in range(SIDE):
        for i in range(3):
            put(i, k, from_y[i][:, k * COLS : (k + 1) * COLS])
        put(3, k, from_z[k][...])
    scale = 1.0 / math.sqrt(WIDTH)
    for n in range(4):
        at = slice(n * 512, (n + 1) * 512)
        product = jnp.dot(clips[...], captions[:, at], preferred_element_type=F32) * scale
        plain[:, at] = product
        ids = lax.broadcasted_iota(jnp.int32, (ROWS, 512), 0)
        raised[:, at] = product + BOOST * (ids == owner[:, at]).astype(F32)

    def peak_body(rows):
        best = plain[rows, tile(0)]
        for t in range(1, TILES):
            best = jnp.maximum(best, plain[rows, tile(t)])
        best = jnp.broadcast_to(jnp.max(best, axis=1, keepdims=True), best.shape) + BOOST
        peaks[rows, :] = best
        sum0 = jnp.zeros_like(best)
        sum1 = jnp.zeros_like(best)
        for t in range(TILES):
            value = plain[rows, tile(t)]
            term = jnp.exp(value - best)
            sum0 += term
            sum1 += jnp.where(raised[rows, tile(t)] > value, term * math.exp(BOOST), term)
        acc0[rows, :] = sum0
        acc1[rows, :] = sum1

    row_chunks(32, peak_body)
    best = jnp.max(jnp.transpose(peaks[...]), axis=0, keepdims=True)
    copy_out(stats, best + jnp.log(jnp.concatenate([along(acc1[...]), along(acc0[...])])))


def first_cols_kernel(raised, plain, parts, row_dual, row_lse, stats):
    row_dual[...] = down(-joined(parts[:, 0, :]))
    row_lse[...] = down(joined(parts[:, 1, :]))
    for t in range(TILES):
        block = raised[:, tile(t)] + row_dual[...]
        best = jnp.max(block, axis=0, keepdims=True)
        total = jnp.sum(jnp.exp(block - best), axis=0, keepdims=True)
        block = plain[:, tile(t)]
        best_plain = jnp.max(block, axis=0, keepdims=True)
        total_plain = jnp.sum(jnp.exp(block - best_plain), axis=0, keepdims=True)
        line = jnp.concatenate([best + jnp.log(total), best_plain + jnp.log(total_plain)])
        for k in range(16):
            stats[k, :, tile(t)] = line


def joint_kernel(raised, row_dual, parts, joint, col_lse, sums, line, acc):
    line[...] = jnp.broadcast_to(HALF_LOG - joined(parts[:, 0, :]), line.shape)
    col_lse[...] = joined(parts[:, 1, :])

    def body(rows):
        dual = row_dual[rows, :]
        total = jnp.zeros_like(dual)
        for t in range(TILES):
            value = jnp.exp(raised[rows, tile(t)] + dual + line[0:1, tile(t)])
            joint[rows, tile(t)] = value
            total += value
        acc[rows, :] = total

    row_chunks(32, body)
    copy_out(sums, along(acc[...]))


def col_step_kernel(joint, parts, sums, scale):
    scale[...] = down(1.0 / gathered(parts))
    for t in range(TILES):
        total = jnp.sum(joint[:, tile(t)] * scale[...], axis=0, keepdims=True)
        for k in range(16):
            sums[k, :, tile(t)] = total


def row_step_kernel(joint, parts, sums, line, acc):
    line[...] = jnp.broadcast_to(0.5 / gathered(parts), line.shape)

    def body(rows):
        total = joint[rows, tile(0)] * line[0:1, tile(0)]
        for t in range(1, TILES):
            total += joint[rows, tile(t)] * line[0:1, tile(t)]
        acc[rows, :] = total

    row_chunks(32, body)
    copy_out(sums, along(acc[...]))


def last_col_kernel(joint, plain, col_lse, parts, scale, sums):
    scale[...] = down(1.0 / gathered(parts))
    for t in range(TILES):
        value = joint[:, tile(t)] * scale[...]
        total = jnp.sum(value, axis=0, keepdims=True)
        gap = col_lse[0:1, tile(t)] - plain[:, tile(t)]
        both = jnp.concatenate([total, jnp.sum(value * gap, axis=0, keepdims=True)])
        for k in range(16):
            sums[k, :, tile(t)] = both


def last_row_kernel(joint, plain, row_lse, parts, col_scale, sums, line, acc0, acc1):
    total = gathered(parts)
    factor = 0.5 / total[0:1]
    col_scale[...] = factor
    line[...] = jnp.broadcast_to(factor, line.shape)
    col_terms = jnp.sum(factor * total[1:2], axis=1, keepdims=True)

    def body(rows):
        lse = row_lse[rows, :]
        sum0 = jnp.zeros_like(lse)
        sum1 = jnp.zeros_like(lse)
        for t in range(TILES):
            value = joint[rows, tile(t)] * line[0:1, tile(t)]
            sum0 += value
            sum1 += value * (lse - plain[rows, tile(t)])
        acc0[rows, :] = sum0
        acc1[rows, :] = sum1

    row_chunks(32, body)
    terms = jnp.broadcast_to(col_terms, (1, ROWS))
    copy_out(sums, jnp.concatenate([along(acc0[...]), along(acc1[...]), terms, terms]))


def chunk_pairs(place, slope, clips_t, i):
    y, z = place[0], place[1]

    def columns(k):
        block = ((y + AWAY[i]) % SIDE) * SIDE + (z + AWAY[k]) % SIDE
        return slope[:, pl.ds(pl.multiple_of(block * LANES, LANES), LANES)]

    for k in (0, 2):
        two = jnp.concatenate([columns(k), columns(k + 1)], axis=1)
        product = jnp.dot(clips_t[...], two, preferred_element_type=F32)
        yield k, product[:, 0:LANES]
        yield k + 1, product[:, LANES:]


def slope_kernel(
    place, joint, plain, row_lse, col_lse, row_scale, col_scale, clips_t, parts, *refs
):
    slope, own_share, *to_y = refs[:4]
    both, line = refs[4:]
    total = gathered(parts)
    norm = 1.0 / total[0:1]
    row_terms = jnp.sum(total[1:2] * norm, axis=1, keepdims=True)
    share = jnp.broadcast_to(row_terms + total[2:3, 0:1] / 16.0, (1, LANES)) / 16384.0
    own_share[...] = share
    both[...] = row_scale[...] + down(norm)
    line[...] = jnp.broadcast_to(col_scale[...], line.shape)

    def body(rows):
        scale = both[rows, :]
        lse = row_lse[rows, :]
        for t in range(TILES):
            value = plain[rows, tile(t)]
            soft = jnp.exp(value - lse) + 0.5 * jnp.exp(value - col_lse[0:1, tile(t)])
            target = joint[rows, tile(t)] * line[0:1, tile(t)] * scale
            slope[rows, tile(t)] = (soft - target).astype(BF16)

    row_chunks(32, body)
    for i in (1, 2):
        for k, product in chunk_pairs(place, slope, clips_t, i):
            narrow(product, share, to_y[i - 1], k * PACKED)

def far_kernel(place, slope, clips_t, share, own_z, *to_z):
    for k, product in chunk_pairs(place, slope, clips_t, 3):
        if k == 0:
            own_z[...] = product
        else:
            narrow(product, share[...], to_z[k - 1], 0)


SHARE = ROWS // 8


def near_kernel(place, slope, clips_t, *own_y):
    for k, value in chunk_pairs(place, slope, clips_t, 0):
        own_y[k][...] = value


def clip_kernel(place, slope, captions, kept, sent, product):
    product[...] = lax.dot_general(
        slope[...], captions[...], (((1,), (1,)), ((), ())), preferred_element_type=F32
    )
    x, core = place[2] // 2, place[2] % 2
    near = x + 1 - 2 * (x % 2)

    def rows_for(core):
        return [
            product[pl.ds(pl.multiple_of((chip * 2 + core) * SHARE, SHARE), SHARE), :]
            for chip in (x, 3 - x, near, 3 - near)
        ]

    kept[...] = jnp.concatenate(rows_for(core))
    narrow(jnp.concatenate(rows_for(1 - core)), ZERO, sent, 0)


def halve_kernel(own, came, kept, sent):
    value = own[...] + widen(came[...])[0]
    half = value.shape[0] // 2
    kept[...] = value[0:half]
    narrow(value[half:], ZERO, sent, 0)


def add_kernel(own, came, out):
    out[...] = own[...] + widen(came[...])[0]


def total(own, own_share, parts):
    value, share = own[...], own_share[...]
    for part in parts:
        more, came = widen(part[...])
        value += more
        share += came
    return value, share


def pass_on_kernel(own, own_share, *refs):
    parts, out = refs[:-1], refs[-1]
    value, share = total(own, own_share, parts)
    narrow(value, share, out, 0)


def keep_kernel(own, own_share, *refs):
    parts, (value_out, share_out) = refs[:-2], refs[-2:]
    value_out[...], share_out[...] = total(own, own_share, parts)


def final_kernel(own_share, kept, *refs):
    parts, (caption_grad, loss) = refs[0:4], refs[4:]
    value, loss[...] = total(kept, own_share, parts)
    caption_grad[...] = jnp.transpose(value)


def body(clips, captions, caption_owner):
    row = lax.axis_index("row").astype(jnp.int32)
    col = lax.axis_index("col").astype(jnp.int32)
    place = jnp.stack([row // SIDE, row % SIDE, col, col])
    owner = (caption_owner - row * ROWS).reshape(1, COLS)
    area = ROWS * COLS

    captions_t = captions.T
    far = row_shift(captions_t, 2, 0)
    from_z = along_z([captions_t] * SIDE)
    beside = swap(clips.T, 2)
    from_z[0], two = call(
        local_kernel,
        [captions_t, clips.T, beside],
        [shape((CAPTION_PIECE, COLS), BF16), shape((2 * CLIP_PIECE, ROWS), BF16)],
        "local",
        moved=2**20,
    )
    far, from_z = lax.optimization_barrier((far, from_z))
    joined = join(from_z)
    clips_here = pair(two, swap(two, 6))
    clips_rows, clips_t = call(
        clips_kernel,
        [place, clips_here, swap(clips_here, 1)],
        [pltpu.VMEM((ROWS, WIDTH), BF16), pltpu.VMEM((WIDTH, ROWS), BF16)],
        "clips",
        smem=1,
        moved=2**21,
    )
    from_y = along_y([joined] * 3)
    from_z = along_z([far] * SIDE)

    captions_full, plain, raised, stats = call(
        logits_kernel,
        [place, owner, clips_rows, *from_z, *from_y],
        [
            pltpu.VMEM((WIDTH, COLS), BF16),
            pltpu.VMEM((ROWS, COLS), F32),
            pltpu.VMEM((ROWS, COLS), F32),
            shape((8, 2, ROWS)),
        ],
        "logits",
        [pltpu.VMEM((ROWS, LANES), F32)] * 3,
        smem=1,
        limit=12,
        flops=2 * area * WIDTH,
        moved=20 * 2**20,
        exps=2 * area,
    )
    parts = col_all(stats)
    row_dual, row_lse, stats = call(
        first_cols_kernel,
        [raised, plain, parts],
        [pltpu.VMEM((ROWS, LANES), F32), pltpu.VMEM((ROWS, LANES), F32), shape((16, 2, COLS))],
        "first_cols",
        flops=6 * area,
        moved=4 * area,
        exps=area,
    )
    parts = row_all(stats)
    joint, col_lse, sums = call(
        joint_kernel,
        [raised, row_dual, parts],
        [pltpu.VMEM((ROWS, COLS), F32), shape((1, COLS)), shape((8, 1, ROWS))],
        "joint",
        [pltpu.VMEM((8, COLS), F32), pltpu.VMEM((ROWS, LANES), F32)],
        flops=6 * area,
        moved=8 * area,
        exps=area,
    )
    parts = col_all(sums)
    (sums,) = call(
        col_step_kernel,
        [joint, parts],
        [shape((16, 1, COLS))],
        "col_step",
        [pltpu.VMEM((ROWS, LANES), F32)],
        flops=2 * area,
        moved=4 * area,
    )
    (sums,) = call(
        row_step_kernel,
        [joint, row_all(sums)],
        [shape((8, 1, ROWS))],
        "row_step",
        [pltpu.VMEM((8, COLS), F32), pltpu.VMEM((ROWS, LANES), F32)],
        flops=2 * area,
        moved=4 * area,
    )
    row_scale, sums = call(
        last_col_kernel,
        [joint, plain, col_lse, col_all(sums)],
        [pltpu.VMEM((ROWS, LANES), F32), shape((16, 2, COLS))],
        "last_col",
        flops=4 * area,
        moved=8 * area,
    )
    col_scale, sums = call(
        last_row_kernel,
        [joint, plain, row_lse, row_all(sums)],
        [shape((1, COLS)), shape((8, 4, ROWS))],
        "last_row",
        [pltpu.VMEM((8, COLS), F32)] + [pltpu.VMEM((ROWS, LANES), F32)] * 2,
        flops=4 * area,
        moved=8 * area,
    )
    def packed(chunks):
        return shape((chunks * PACKED, LANES), jnp.int16)

    slope, share, *to_y = call(
        slope_kernel,
        [place, joint, plain, row_lse, col_lse, row_scale, col_scale, clips_t, col_all(sums)],
        [pltpu.VMEM((ROWS, COLS), BF16), shape((1, LANES))] + [packed(SIDE)] * 2,
        "slope",
        [pltpu.VMEM((ROWS, LANES), F32), pltpu.VMEM((8, COLS), F32)],
        smem=1,
        flops=area * WIDTH,
        moved=12 * area,
        exps=2 * area,
    )
    from_y = along_y([None, *to_y])[1:]
    own_z, *to_z = call(
        far_kernel,
        [place, slope, clips_t, share],
        [shape((WIDTH, LANES))] + [packed(1)] * 3,
        "far",
        smem=1,
        flops=area * WIDTH // 2,
        moved=8 * area,
    )
    two_away = row_shift(to_z[2], 0, 2)
    from_z = [row_shift(to_z[0], 0, 1), row_shift(to_z[1], 0, 3), two_away]
    own_z, slope = lax.optimization_barrier((own_z, slope))
    clip_own, sent = call(
        clip_kernel,
        [place, slope, captions_full],
        [shape((4 * SHARE, WIDTH)), shape((4 * SHARE + EXTRA, WIDTH), jnp.int16)],
        "clip_share",
        [pltpu.VMEM((ROWS, WIDTH), F32)],
        smem=1,
        flops=2 * area * WIDTH,
        moved=8 * area,
    )
    came = swap(sent, 1)
    own_y0, own_y1, own_y2, own_y3 = call(
        near_kernel,
        [place, slope, clips_t],
        [shape((WIDTH, LANES))] * 4,
        "near",
        smem=1,
        flops=area * WIDTH // 2,
        moved=4 * area,
    )
    came, own_y0 = lax.optimization_barrier((came, own_y0))
    from_y, came_z = lax.optimization_barrier((from_y, from_z))
    from_z, all_sent = [], []
    for k, own in ((1, own_y1), (2, own_y2), (3, own_y3)):
        chunk = pl.BlockSpec((PACKED, LANES), lambda step, k=k: (k, 0))
        (sent_z,) = call(
            pass_on_kernel,
            [own, share, *from_y],
            [packed(1)],
            "pass_on_z",
            moved=2**21,
            specs=[VM, VM, chunk, chunk],
            grid=(1,),
        )
        all_sent.append(sent_z)
        from_z.append(row_shift(sent_z, 0, AWAY[k]))
    (sent_on,) = call(pass_on_kernel, [own_z, share, *came_z], [packed(1)], "pass_on_y", moved=2**21)
    from_y2 = row_shift(sent_on, 2, 0)
    chunk = pl.BlockSpec((PACKED, LANES), lambda step: (0, 0))
    kept, share = call(
        keep_kernel,
        [own_y0, share, *from_y],
        [shape((WIDTH, LANES)), shape((1, LANES))],
        "keep",
        moved=2**21,
        specs=[VM, VM, chunk, chunk],
        grid=(1,),
    )
    for rows, bits in ((2 * SHARE, 2), (SHARE, 6)):
        clip_own, sent = call(
            halve_kernel,
            [clip_own, came],
            [shape((rows, WIDTH)), shape((rows + EXTRA, WIDTH), jnp.int16)],
            "halve",
            moved=2**21,
        )
        came = swap(sent, bits)
    (clip_grad,) = call(add_kernel, [clip_own, came], [shape((SHARE, WIDTH))], "clip_add")
    clip_grad, kept = lax.optimization_barrier((clip_grad, kept))
    caption_grad, loss = call(
        final_kernel,
        [share, kept, from_y2, *from_z],
        [shape((LANES, WIDTH)), shape((1, LANES))],
        "final",
        flops=area,
        moved=4 * area,
    )
    return loss[0, 0], clip_grad, caption_grad


def solution(mesh):
    in_specs = (P("row", "col"), P("col", "row"), P("col"))
    out_specs = (P(), P(("row", "col"), None), P(("col", "row"), None))
    return jax.shard_map(body, mesh=mesh, in_specs=in_specs, out_specs=out_specs, check_vma=False)
```

```python
import math

import jax
import jax.numpy as jnp
from jax import lax
from jax.experimental import pallas as pl
from jax.experimental.pallas import tpu as pltpu
from jax.sharding import PartitionSpec as P

BOOST = 4.0
HALF_LOG = math.log(0.5)
WIDTH = 768
ROWS = 512
COLS = 2048
LANES = 128
TILES = COLS // LANES
SIDE = 4
CLIP_PIECE = 96
CAPTION_PIECE = 48
EXTRA = 16
PACKED = WIDTH + EXTRA
AWAY = (0, 1, 3, 2)
F32 = jnp.float32
BF16 = jnp.bfloat16

VM = pl.BlockSpec(memory_space=pltpu.VMEM)
SM = pl.BlockSpec(memory_space=pltpu.SMEM)


def call(
    kernel, args, outs, name, scratch=(), smem=0, limit=8, flops=0, moved=0, exps=0, specs=None, grid=()
):
    return pl.pallas_call(
        kernel,
        grid=grid,
        out_shape=outs,
        in_specs=specs or [SM] * smem + [VM] * (len(args) - smem),
        out_specs=[VM] * len(outs),
        scratch_shapes=list(scratch),
        compiler_params=pltpu.CompilerParams(vmem_limit_bytes=limit * 2**20),
        cost_estimate=pl.CostEstimate(flops=flops, bytes_accessed=moved, transcendentals=exps),
        name=name,
    )(*args)


def shape(dims, kind=F32):
    return jax.ShapeDtypeStruct(dims, kind)


def row_shift(value, step_y, step_z):
    pairs = [
        (y * SIDE + z, ((y + step_y) % SIDE) * SIDE + (z + step_z) % SIDE)
        for y in range(SIDE)
        for z in range(SIDE)
    ]
    return lax.ppermute(value, "row", pairs)


def col_shift(value, step_x, flip):
    pairs = [
        (x * 2 + k, ((x + step_x) % SIDE) * 2 + (k ^ flip)) for x in range(SIDE) for k in range(2)
    ]
    return lax.ppermute(value, "col", pairs)


AWAY = (0, 1, 3, 2)


def col_all(copies):
    return lax.all_to_all(copies, "col", 0, 0, tiled=True)


def row_all(copies):
    return lax.all_to_all(copies, "row", 0, 0, tiled=True)


def swap(value, bits):
    return lax.ppermute(value, "col", [(c, c ^ bits) for c in range(8)])


def along_z(values):
    return [values[0]] + [row_shift(v, 0, d) for v, d in zip(values[1:], AWAY[1:])]


def along_y(values):
    return [values[0]] + [row_shift(v, d, 0) for v, d in zip(values[1:], AWAY[1:])]


def down(line):
    return jnp.transpose(jnp.broadcast_to(line, (LANES, line.shape[1])))


def along(block):
    return jnp.sum(jnp.transpose(block), axis=0, keepdims=True)


def copy_out(sums, value):
    for k in range(sums.shape[0]):
        sums[k] = value


def integers(packed):
    return packed.astype(jnp.int32).astype(F32)


def scale_of(steps):
    return jnp.exp2(steps * (1 / 64)) * (1 / 32000)


def steps_of(peak):
    return jnp.ceil(jnp.log2(jnp.maximum(peak, 1e-30)) * 64.0)


def halfwords(numbers):
    return jnp.round(numbers).astype(jnp.int32).astype(jnp.int16)


def widen(packed):
    rows = packed.shape[0] - EXTRA
    tail = integers(packed[rows:])
    share = (tail[2:3] + tail[3:4] * 2.0**-14) * scale_of(tail[1:2])
    return integers(packed[0:rows]) * scale_of(tail[0:1]), share


ZERO = 0.0


def narrow(value, share, out, start):
    rows, lanes = value.shape
    steps = steps_of(jnp.max(jnp.abs(value), axis=0, keepdims=True))
    out[start : start + rows] = halfwords(value * (1.0 / scale_of(steps)))
    share = share + jnp.zeros((1, lanes), F32)
    share_steps = steps_of(jnp.abs(share))
    scaled = share * (1.0 / scale_of(share_steps))
    high = jnp.round(scaled)
    low = (scaled - high) * 2.0**14
    row = lax.broadcasted_iota(jnp.int32, (EXTRA, lanes), 0)
    tail = jnp.where(
        row == 0, steps, jnp.where(row == 1, share_steps, jnp.where(row == 2, high, low))
    )
    out[start + rows : start + rows + EXTRA] = halfwords(tail)


def gathered(parts):
    total = parts[0]
    for k in range(1, parts.shape[0]):
        total += parts[k]
    return total


def joined(lses):
    peak = jnp.max(lses, axis=0, keepdims=True)
    return peak + jnp.log(jnp.sum(jnp.exp(lses - peak), axis=0, keepdims=True))


def tile(t):
    return slice(t * LANES, (t + 1) * LANES)


def row_chunks(step, body):
    def run(i, carry):
        body(pl.ds(pl.multiple_of(i * step, step), step))
        return carry

    lax.fori_loop(0, ROWS // step, run, 0)


def local_kernel(captions, clips, beside, captions_out, clips_out):
    captions_out[...] = captions[...]
    clips_out[0:CLIP_PIECE] = clips[...]
    clips_out[CLIP_PIECE:] = beside[...]


def join_kernel(*refs):
    parts, out = refs[:-1], refs[-1]
    for k, part in enumerate(parts):
        out[:, k * COLS : (k + 1) * COLS] = part[...]


def join(parts):
    dims = (CAPTION_PIECE, len(parts) * COLS)
    return call(join_kernel, parts, [shape(dims, BF16)], "join", moved=2**21)[0]


def pair_kernel(first, second, out):
    rows = first.shape[0]
    out[0:rows] = first[...]
    out[rows:] = second[...]


def pair(first, second):
    dims = (2 * first.shape[0], ROWS)
    return call(pair_kernel, [first, second], [shape(dims, BF16)], "pair", moved=2**20)[0]


def clips_kernel(place, here, there, clips, clips_t):
    x, core = place[2] // 2, place[2] % 2
    near = x + 1 - 2 * (x % 2)
    for k, part in enumerate((here, there)):
        for i, chip in enumerate((x, near, 3 - x, 3 - near)):
            rows = pl.ds(pl.multiple_of((2 * chip + (core + k) % 2) * CLIP_PIECE, 16), CLIP_PIECE)
            clips_t[rows, :] = part[i * CLIP_PIECE : (i + 1) * CLIP_PIECE]
    clips[...] = jnp.transpose(clips_t[...])


def logits_kernel(place, owner, clips, *refs):
    from_z, from_y, outs, (acc0, acc1, peaks) = refs[:4], refs[4:7], refs[7:11], refs[11:]
    captions, plain, raised, stats = outs
    y, z = place[0], place[1]

    def put(i, k, piece):
        block = ((y - AWAY[i] + SIDE) % SIDE) * SIDE + (z - AWAY[k] + SIDE) % SIDE
        rows = pl.ds(pl.multiple_of(block * CAPTION_PIECE, 16), CAPTION_PIECE)
        captions[rows, :] = piece

    for k in range(SIDE):
        for i in range(3):
            put(i, k, from_y[i][:, k * COLS : (k + 1) * COLS])
        put(3, k, from_z[k][...])
    scale = 1.0 / math.sqrt(WIDTH)
    for n in range(4):
        at = slice(n * 512, (n + 1) * 512)
        product = jnp.dot(clips[...], captions[:, at], preferred_element_type=F32) * scale
        plain[:, at] = product
        ids = lax.broadcasted_iota(jnp.int32, (ROWS, 512), 0)
        raised[:, at] = product + BOOST * (ids == owner[:, at]).astype(F32)

    def peak_body(rows):
        best = plain[rows, tile(0)]
        for t in range(1, TILES):
            best = jnp.maximum(best, plain[rows, tile(t)])
        best = jnp.broadcast_to(jnp.max(best, axis=1, keepdims=True), best.shape) + BOOST
        peaks[rows, :] = best
        sum0 = jnp.zeros_like(best)
        sum1 = jnp.zeros_like(best)
        for t in range(TILES):
            value = plain[rows, tile(t)]
            term = jnp.exp(value - best)
            sum0 += term
            sum1 += jnp.where(raised[rows, tile(t)] > value, term * math.exp(BOOST), term)
        acc0[rows, :] = sum0
        acc1[rows, :] = sum1

    row_chunks(32, peak_body)
    best = jnp.max(jnp.transpose(peaks[...]), axis=0, keepdims=True)
    copy_out(stats, best + jnp.log(jnp.concatenate([along(acc1[...]), along(acc0[...])])))


def first_cols_kernel(raised, plain, parts, row_dual, row_lse, stats):
    row_dual[...] = down(-joined(parts[:, 0, :]))
    row_lse[...] = down(joined(parts[:, 1, :]))
    for t in range(TILES):
        block = raised[:, tile(t)] + row_dual[...]
        best = jnp.max(block, axis=0, keepdims=True)
        total = jnp.sum(jnp.exp(block - best), axis=0, keepdims=True)
        block = plain[:, tile(t)]
        best_plain = jnp.max(block, axis=0, keepdims=True)
        total_plain = jnp.sum(jnp.exp(block - best_plain), axis=0, keepdims=True)
        line = jnp.concatenate([best + jnp.log(total), best_plain + jnp.log(total_plain)])
        for k in range(16):
            stats[k, :, tile(t)] = line


def joint_kernel(raised, row_dual, parts, joint, col_lse, sums, line, acc):
    line[...] = jnp.broadcast_to(HALF_LOG - joined(parts[:, 0, :]), line.shape)
    col_lse[...] = joined(parts[:, 1, :])

    def body(rows):
        dual = row_dual[rows, :]
        total = jnp.zeros_like(dual)
        for t in range(TILES):
            value = jnp.exp(raised[rows, tile(t)] + dual + line[0:1, tile(t)])
            joint[rows, tile(t)] = value
            total += value
        acc[rows, :] = total

    row_chunks(32, body)
    copy_out(sums, along(acc[...]))


def col_step_kernel(joint, parts, sums, scale):
    scale[...] = down(1.0 / gathered(parts))
    for t in range(TILES):
        total = jnp.sum(joint[:, tile(t)] * scale[...], axis=0, keepdims=True)
        for k in range(16):
            sums[k, :, tile(t)] = total


def row_step_kernel(joint, parts, sums, line, acc):
    line[...] = jnp.broadcast_to(0.5 / gathered(parts), line.shape)

    def body(rows):
        total = joint[rows, tile(0)] * line[0:1, tile(0)]
        for t in range(1, TILES):
            total += joint[rows, tile(t)] * line[0:1, tile(t)]
        acc[rows, :] = total

    row_chunks(32, body)
    copy_out(sums, along(acc[...]))


def last_col_kernel(joint, plain, col_lse, parts, scale, sums):
    scale[...] = down(1.0 / gathered(parts))
    for t in range(TILES):
        value = joint[:, tile(t)] * scale[...]
        total = jnp.sum(value, axis=0, keepdims=True)
        gap = col_lse[0:1, tile(t)] - plain[:, tile(t)]
        both = jnp.concatenate([total, jnp.sum(value * gap, axis=0, keepdims=True)])
        for k in range(16):
            sums[k, :, tile(t)] = both


def last_row_kernel(joint, plain, row_lse, parts, col_scale, sums, line, acc0, acc1):
    total = gathered(parts)
    factor = 0.5 / total[0:1]
    col_scale[...] = factor
    line[...] = jnp.broadcast_to(factor, line.shape)
    col_terms = jnp.sum(factor * total[1:2], axis=1, keepdims=True)

    def body(rows):
        lse = row_lse[rows, :]
        sum0 = jnp.zeros_like(lse)
        sum1 = jnp.zeros_like(lse)
        for t in range(TILES):
            value = joint[rows, tile(t)] * line[0:1, tile(t)]
            sum0 += value
            sum1 += value * (lse - plain[rows, tile(t)])
        acc0[rows, :] = sum0
        acc1[rows, :] = sum1

    row_chunks(32, body)
    terms = jnp.broadcast_to(col_terms, (1, ROWS))
    copy_out(sums, jnp.concatenate([along(acc0[...]), along(acc1[...]), terms, terms]))


def chunk_pairs(place, slope, clips_t, i):
    y, z = place[0], place[1]

    def columns(k):
        block = ((y + AWAY[i]) % SIDE) * SIDE + (z + AWAY[k]) % SIDE
        return slope[:, pl.ds(pl.multiple_of(block * LANES, LANES), LANES)]

    for k in (0, 2):
        two = jnp.concatenate([columns(k), columns(k + 1)], axis=1)
        product = jnp.dot(clips_t[...], two, preferred_element_type=F32)
        yield k, product[:, 0:LANES]
        yield k + 1, product[:, LANES:]


def slope_kernel(
    place, joint, plain, row_lse, col_lse, row_scale, col_scale, clips_t, parts, *refs
):
    slope, own_share, *to_y = refs[:4]
    both, line = refs[4:]
    total = gathered(parts)
    norm = 1.0 / total[0:1]
    row_terms = jnp.sum(total[1:2] * norm, axis=1, keepdims=True)
    share = jnp.broadcast_to(row_terms + total[2:3, 0:1] / 16.0, (1, LANES)) / 16384.0
    own_share[...] = share
    both[...] = row_scale[...] + down(norm)
    line[...] = jnp.broadcast_to(col_scale[...], line.shape)

    def body(rows):
        scale = both[rows, :]
        lse = row_lse[rows, :]
        for t in range(TILES):
            value = plain[rows, tile(t)]
            soft = jnp.exp(value - lse) + 0.5 * jnp.exp(value - col_lse[0:1, tile(t)])
            target = joint[rows, tile(t)] * line[0:1, tile(t)] * scale
            slope[rows, tile(t)] = (soft - target).astype(BF16)

    row_chunks(32, body)
    for i in (1, 2):
        for k, product in chunk_pairs(place, slope, clips_t, i):
            narrow(product, share, to_y[i - 1], k * PACKED)

def far_kernel(place, slope, clips_t, share, own_z, *to_z):
    for k, product in chunk_pairs(place, slope, clips_t, 3):
        if k == 0:
            own_z[...] = product
        else:
            narrow(product, share[...], to_z[k - 1], 0)


SHARE = ROWS // 8


def near_kernel(place, slope, clips_t, *own_y):
    for k, value in chunk_pairs(place, slope, clips_t, 0):
        own_y[k][...] = value


def clip_kernel(place, slope, captions, kept, sent, product):
    product[...] = lax.dot_general(
        slope[...], captions[...], (((1,), (1,)), ((), ())), preferred_element_type=F32
    )
    x, core = place[2] // 2, place[2] % 2
    near = x + 1 - 2 * (x % 2)

    def rows_for(core):
        return [
            product[pl.ds(pl.multiple_of((chip * 2 + core) * SHARE, SHARE), SHARE), :]
            for chip in (x, 3 - x, near, 3 - near)
        ]

    kept[...] = jnp.concatenate(rows_for(core))
    narrow(jnp.concatenate(rows_for(1 - core)), ZERO, sent, 0)


def halve_kernel(own, came, kept, sent):
    value = own[...] + widen(came[...])[0]
    half = value.shape[0] // 2
    kept[...] = value[0:half]
    narrow(value[half:], ZERO, sent, 0)


def add_kernel(own, came, out):
    out[...] = own[...] + widen(came[...])[0]


def total(own, own_share, parts):
    value, share = own[...], own_share[...]
    for part in parts:
        more, came = widen(part[...])
        value += more
        share += came
    return value, share


def pass_on_kernel(own, own_share, *refs):
    parts, out = refs[:-1], refs[-1]
    value, share = total(own, own_share, parts)
    narrow(value, share, out, 0)


def keep_kernel(own, own_share, *refs):
    parts, (value_out, share_out) = refs[:-2], refs[-2:]
    value_out[...], share_out[...] = total(own, own_share, parts)


def final_kernel(own_share, kept, *refs):
    parts, (caption_grad, loss) = refs[0:4], refs[4:]
    value, loss[...] = total(kept, own_share, parts)
    caption_grad[...] = jnp.transpose(value)


def body(clips, captions, caption_owner):
    row = lax.axis_index("row").astype(jnp.int32)
    col = lax.axis_index("col").astype(jnp.int32)
    place = jnp.stack([row // SIDE, row % SIDE, col, col])
    owner = (caption_owner - row * ROWS).reshape(1, COLS)
    area = ROWS * COLS

    captions_t = captions.T
    far = row_shift(captions_t, 2, 0)
    from_z = along_z([captions_t] * SIDE)
    beside = swap(clips.T, 2)
    from_z[0], two = call(
        local_kernel,
        [captions_t, clips.T, beside],
        [shape((CAPTION_PIECE, COLS), BF16), shape((2 * CLIP_PIECE, ROWS), BF16)],
        "local",
        flops=2**33,
        moved=2**20,
    )
    far, from_z = lax.optimization_barrier((far, from_z))
    joined = join(from_z)
    clips_here = pair(two, swap(two, 6))
    clips_rows, clips_t = call(
        clips_kernel,
        [place, clips_here, swap(clips_here, 1)],
        [pltpu.VMEM((ROWS, WIDTH), BF16), pltpu.VMEM((WIDTH, ROWS), BF16)],
        "clips",
        smem=1,
        moved=2**21,
    )
    from_y = along_y([joined] * 3)
    from_z = along_z([far] * SIDE)

    captions_full, plain, raised, stats = call(
        logits_kernel,
        [place, owner, clips_rows, *from_z, *from_y],
        [
            pltpu.VMEM((WIDTH, COLS), BF16),
            pltpu.VMEM((ROWS, COLS), F32),
            pltpu.VMEM((ROWS, COLS), F32),
            shape((8, 2, ROWS)),
        ],
        "logits",
        [pltpu.VMEM((ROWS, LANES), F32)] * 3,
        smem=1,
        limit=12,
        flops=2 * area * WIDTH,
        moved=20 * 2**20,
        exps=2 * area,
    )
    parts = col_all(stats)
    row_dual, row_lse, stats = call(
        first_cols_kernel,
        [raised, plain, parts],
        [pltpu.VMEM((ROWS, LANES), F32), pltpu.VMEM((ROWS, LANES), F32), shape((16, 2, COLS))],
        "first_cols",
        flops=6 * area,
        moved=4 * area,
        exps=area,
    )
    parts = row_all(stats)
    joint, col_lse, sums = call(
        joint_kernel,
        [raised, row_dual, parts],
        [pltpu.VMEM((ROWS, COLS), F32), shape((1, COLS)), shape((8, 1, ROWS))],
        "joint",
        [pltpu.VMEM((8, COLS), F32), pltpu.VMEM((ROWS, LANES), F32)],
        flops=6 * area,
        moved=8 * area,
        exps=area,
    )
    parts = col_all(sums)
    (sums,) = call(
        col_step_kernel,
        [joint, parts],
        [shape((16, 1, COLS))],
        "col_step",
        [pltpu.VMEM((ROWS, LANES), F32)],
        flops=2 * area,
        moved=4 * area,
    )
    (sums,) = call(
        row_step_kernel,
        [joint, row_all(sums)],
        [shape((8, 1, ROWS))],
        "row_step",
        [pltpu.VMEM((8, COLS), F32), pltpu.VMEM((ROWS, LANES), F32)],
        flops=2 * area,
        moved=4 * area,
    )
    row_scale, sums = call(
        last_col_kernel,
        [joint, plain, col_lse, col_all(sums)],
        [pltpu.VMEM((ROWS, LANES), F32), shape((16, 2, COLS))],
        "last_col",
        flops=4 * area,
        moved=8 * area,
    )
    col_scale, sums = call(
        last_row_kernel,
        [joint, plain, row_lse, row_all(sums)],
        [shape((1, COLS)), shape((8, 4, ROWS))],
        "last_row",
        [pltpu.VMEM((8, COLS), F32)] + [pltpu.VMEM((ROWS, LANES), F32)] * 2,
        flops=4 * area,
        moved=8 * area,
    )
    def packed(chunks):
        return shape((chunks * PACKED, LANES), jnp.int16)

    slope, share, *to_y = call(
        slope_kernel,
        [place, joint, plain, row_lse, col_lse, row_scale, col_scale, clips_t, col_all(sums)],
        [pltpu.VMEM((ROWS, COLS), BF16), shape((1, LANES))] + [packed(SIDE)] * 2,
        "slope",
        [pltpu.VMEM((ROWS, LANES), F32), pltpu.VMEM((8, COLS), F32)],
        smem=1,
        flops=area * WIDTH,
        moved=12 * area,
        exps=2 * area,
    )
    from_y = along_y([None, *to_y])[1:]
    own_z, *to_z = call(
        far_kernel,
        [place, slope, clips_t, share],
        [shape((WIDTH, LANES))] + [packed(1)] * 3,
        "far",
        smem=1,
        flops=area * WIDTH // 2,
        moved=8 * area,
    )
    two_away = row_shift(to_z[2], 0, 2)
    from_z = [row_shift(to_z[0], 0, 1), row_shift(to_z[1], 0, 3), two_away]
    own_z, slope = lax.optimization_barrier((own_z, slope))
    clip_own, sent = call(
        clip_kernel,
        [place, slope, captions_full],
        [shape((4 * SHARE, WIDTH)), shape((4 * SHARE + EXTRA, WIDTH), jnp.int16)],
        "clip_share",
        [pltpu.VMEM((ROWS, WIDTH), F32)],
        smem=1,
        flops=2 * area * WIDTH,
        moved=8 * area,
    )
    came = swap(sent, 1)
    own_y0, own_y1, own_y2, own_y3 = call(
        near_kernel,
        [place, slope, clips_t],
        [shape((WIDTH, LANES))] * 4,
        "near",
        smem=1,
        flops=area * WIDTH // 2,
        moved=4 * area,
    )
    came, own_y0 = lax.optimization_barrier((came, own_y0))
    from_y, came_z = lax.optimization_barrier((from_y, from_z))
    from_z, all_sent = [], []
    for k, own in ((1, own_y1), (2, own_y2), (3, own_y3)):
        chunk = pl.BlockSpec((PACKED, LANES), lambda step, k=k: (k, 0))
        (sent_z,) = call(
            pass_on_kernel,
            [own, share, *from_y],
            [packed(1)],
            "pass_on_z",
            moved=2**21,
            specs=[VM, VM, chunk, chunk],
            grid=(1,),
        )
        all_sent.append(sent_z)
        from_z.append(row_shift(sent_z, 0, AWAY[k]))
    (sent_on,) = call(pass_on_kernel, [own_z, share, *came_z], [packed(1)], "pass_on_y", moved=2**21)
    from_y2 = row_shift(sent_on, 2, 0)
    chunk = pl.BlockSpec((PACKED, LANES), lambda step: (0, 0))
    kept, share = call(
        keep_kernel,
        [own_y0, share, *from_y],
        [shape((WIDTH, LANES)), shape((1, LANES))],
        "keep",
        moved=2**21,
        specs=[VM, VM, chunk, chunk],
        grid=(1,),
    )
    for rows, bits in ((2 * SHARE, 2), (SHARE, 6)):
        clip_own, sent = call(
            halve_kernel,
            [clip_own, came],
            [shape((rows, WIDTH)), shape((rows + EXTRA, WIDTH), jnp.int16)],
            "halve",
            moved=2**21,
        )
        came = swap(sent, bits)
    (clip_grad,) = call(add_kernel, [clip_own, came], [shape((SHARE, WIDTH))], "clip_add")
    clip_grad, kept = lax.optimization_barrier((clip_grad, kept))
    caption_grad, loss = call(
        final_kernel,
        [share, kept, from_y2, *from_z],
        [shape((LANES, WIDTH)), shape((1, LANES))],
        "final",
        flops=area,
        moved=4 * area,
    )
    return loss[0, 0], clip_grad, caption_grad


def solution(mesh):
    in_specs = (P("row", "col"), P("col", "row"), P("col"))
    out_specs = (P(), P(("row", "col"), None), P(("col", "row"), None))
    return jax.shard_map(body, mesh=mesh, in_specs=in_specs, out_specs=out_specs, check_vma=False)
```

```python
import math

import jax
import jax.numpy as jnp
from jax import lax
from jax.experimental import pallas as pl
from jax.experimental.pallas import tpu as pltpu
from jax.sharding import PartitionSpec as P

BOOST = 4.0
HALF_LOG = math.log(0.5)
WIDTH = 768
ROWS = 512
COLS = 2048
LANES = 128
TILES = COLS // LANES
SIDE = 4
CLIP_PIECE = 96
CAPTION_PIECE = 48
EXTRA = 16
PACKED = WIDTH + EXTRA
AWAY = (0, 1, 3, 2)
F32 = jnp.float32
BF16 = jnp.bfloat16

VM = pl.BlockSpec(memory_space=pltpu.VMEM)
SM = pl.BlockSpec(memory_space=pltpu.SMEM)


def call(
    kernel, args, outs, name, scratch=(), smem=0, limit=8, flops=0, moved=0, exps=0, specs=None, grid=()
):
    return pl.pallas_call(
        kernel,
        grid=grid,
        out_shape=outs,
        in_specs=specs or [SM] * smem + [VM] * (len(args) - smem),
        out_specs=[VM] * len(outs),
        scratch_shapes=list(scratch),
        compiler_params=pltpu.CompilerParams(vmem_limit_bytes=limit * 2**20),
        cost_estimate=pl.CostEstimate(flops=flops, bytes_accessed=moved, transcendentals=exps),
        name=name,
    )(*args)


def shape(dims, kind=F32):
    return jax.ShapeDtypeStruct(dims, kind)


def row_shift(value, step_y, step_z):
    pairs = [
        (y * SIDE + z, ((y + step_y) % SIDE) * SIDE + (z + step_z) % SIDE)
        for y in range(SIDE)
        for z in range(SIDE)
    ]
    return lax.ppermute(value, "row", pairs)


def col_shift(value, step_x, flip):
    pairs = [
        (x * 2 + k, ((x + step_x) % SIDE) * 2 + (k ^ flip)) for x in range(SIDE) for k in range(2)
    ]
    return lax.ppermute(value, "col", pairs)


AWAY = (0, 1, 3, 2)


def col_all(copies):
    return lax.all_to_all(copies, "col", 0, 0, tiled=True)


def row_all(copies):
    return lax.all_to_all(copies, "row", 0, 0, tiled=True)


def swap(value, bits):
    return lax.ppermute(value, "col", [(c, c ^ bits) for c in range(8)])


def along_z(values):
    return [values[0]] + [row_shift(v, 0, d) for v, d in zip(values[1:], AWAY[1:])]


def along_y(values):
    return [values[0]] + [row_shift(v, d, 0) for v, d in zip(values[1:], AWAY[1:])]


def down(line):
    return jnp.transpose(jnp.broadcast_to(line, (LANES, line.shape[1])))


def along(block):
    return jnp.sum(jnp.transpose(block), axis=0, keepdims=True)


def copy_out(sums, value):
    for k in range(sums.shape[0]):
        sums[k] = value


def integers(packed):
    return packed.astype(jnp.int32).astype(F32)


def scale_of(steps):
    return jnp.exp2(steps * (1 / 64)) * (1 / 32000)


def steps_of(peak):
    return jnp.ceil(jnp.log2(jnp.maximum(peak, 1e-30)) * 64.0)


def halfwords(numbers):
    return jnp.round(numbers).astype(jnp.int32).astype(jnp.int16)


def widen(packed):
    rows = packed.shape[0] - EXTRA
    tail = integers(packed[rows:])
    share = (tail[2:3] + tail[3:4] * 2.0**-14) * scale_of(tail[1:2])
    return integers(packed[0:rows]) * scale_of(tail[0:1]), share


ZERO = 0.0


def narrow(value, share, out, start):
    rows, lanes = value.shape
    steps = steps_of(jnp.max(jnp.abs(value), axis=0, keepdims=True))
    out[start : start + rows] = halfwords(value * (1.0 / scale_of(steps)))
    share = share + jnp.zeros((1, lanes), F32)
    share_steps = steps_of(jnp.abs(share))
    scaled = share * (1.0 / scale_of(share_steps))
    high = jnp.round(scaled)
    low = (scaled - high) * 2.0**14
    row = lax.broadcasted_iota(jnp.int32, (EXTRA, lanes), 0)
    tail = jnp.where(
        row == 0, steps, jnp.where(row == 1, share_steps, jnp.where(row == 2, high, low))
    )
    out[start + rows : start + rows + EXTRA] = halfwords(tail)


def gathered(parts):
    total = parts[0]
    for k in range(1, parts.shape[0]):
        total += parts[k]
    return total


def joined(lses):
    peak = jnp.max(lses, axis=0, keepdims=True)
    return peak + jnp.log(jnp.sum(jnp.exp(lses - peak), axis=0, keepdims=True))


def tile(t):
    return slice(t * LANES, (t + 1) * LANES)


def row_chunks(step, body):
    def run(i, carry):
        body(pl.ds(pl.multiple_of(i * step, step), step))
        return carry

    lax.fori_loop(0, ROWS // step, run, 0)


def local_kernel(captions, clips, beside, captions_out, clips_out):
    captions_out[...] = captions[...]
    clips_out[0:CLIP_PIECE] = clips[...]
    clips_out[CLIP_PIECE:] = beside[...]


def join_kernel(*refs):
    parts, out = refs[:-1], refs[-1]
    for k, part in enumerate(parts):
        out[:, k * COLS : (k + 1) * COLS] = part[...]


def join(parts):
    dims = (CAPTION_PIECE, len(parts) * COLS)
    return call(join_kernel, parts, [shape(dims, BF16)], "join", moved=2**21)[0]


def pair_kernel(first, second, out):
    rows = first.shape[0]
    out[0:rows] = first[...]
    out[rows:] = second[...]


def pair(first, second):
    dims = (2 * first.shape[0], ROWS)
    return call(pair_kernel, [first, second], [shape(dims, BF16)], "pair", moved=2**20)[0]


def clips_kernel(place, here, there, clips, clips_t):
    x, core = place[2] // 2, place[2] % 2
    near = x + 1 - 2 * (x % 2)
    for k, part in enumerate((here, there)):
        for i, chip in enumerate((x, near, 3 - x, 3 - near)):
            rows = pl.ds(pl.multiple_of((2 * chip + (core + k) % 2) * CLIP_PIECE, 16), CLIP_PIECE)
            clips_t[rows, :] = part[i * CLIP_PIECE : (i + 1) * CLIP_PIECE]
    clips[...] = jnp.transpose(clips_t[...])


def logits_kernel(place, owner, clips, *refs):
    from_z, from_y, outs, (acc0, acc1, peaks) = refs[:4], refs[4:7], refs[7:11], refs[11:]
    captions, plain, raised, stats = outs
    y, z = place[0], place[1]

    def put(i, k, piece):
        block = ((y - AWAY[i] + SIDE) % SIDE) * SIDE + (z - AWAY[k] + SIDE) % SIDE
        rows = pl.ds(pl.multiple_of(block * CAPTION_PIECE, 16), CAPTION_PIECE)
        captions[rows, :] = piece

    for k in range(SIDE):
        for i in range(3):
            put(i, k, from_y[i][:, k * COLS : (k + 1) * COLS])
        put(3, k, from_z[k][...])
    scale = 1.0 / math.sqrt(WIDTH)
    for n in range(4):
        at = slice(n * 512, (n + 1) * 512)
        product = jnp.dot(clips[...], captions[:, at], preferred_element_type=F32) * scale
        plain[:, at] = product
        ids = lax.broadcasted_iota(jnp.int32, (ROWS, 512), 0)
        raised[:, at] = product + BOOST * (ids == owner[:, at]).astype(F32)

    def peak_body(rows):
        best = plain[rows, tile(0)]
        for t in range(1, TILES):
            best = jnp.maximum(best, plain[rows, tile(t)])
        best = jnp.broadcast_to(jnp.max(best, axis=1, keepdims=True), best.shape) + BOOST
        peaks[rows, :] = best
        sum0 = jnp.zeros_like(best)
        sum1 = jnp.zeros_like(best)
        for t in range(TILES):
            value = plain[rows, tile(t)]
            term = jnp.exp(value - best)
            sum0 += term
            sum1 += jnp.where(raised[rows, tile(t)] > value, term * math.exp(BOOST), term)
        acc0[rows, :] = sum0
        acc1[rows, :] = sum1

    row_chunks(32, peak_body)
    best = jnp.max(jnp.transpose(peaks[...]), axis=0, keepdims=True)
    copy_out(stats, best + jnp.log(jnp.concatenate([along(acc1[...]), along(acc0[...])])))


def first_cols_kernel(raised, plain, parts, row_dual, row_lse, stats):
    row_dual[...] = down(-joined(parts[:, 0, :]))
    row_lse[...] = down(joined(parts[:, 1, :]))
    for t in range(TILES):
        block = raised[:, tile(t)] + row_dual[...]
        best = jnp.max(block, axis=0, keepdims=True)
        total = jnp.sum(jnp.exp(block - best), axis=0, keepdims=True)
        block = plain[:, tile(t)]
        best_plain = jnp.max(block, axis=0, keepdims=True)
        total_plain = jnp.sum(jnp.exp(block - best_plain), axis=0, keepdims=True)
        line = jnp.concatenate([best + jnp.log(total), best_plain + jnp.log(total_plain)])
        for k in range(16):
            stats[k, :, tile(t)] = line


def joint_kernel(raised, row_dual, parts, joint, col_lse, sums, line, acc):
    line[...] = jnp.broadcast_to(HALF_LOG - joined(parts[:, 0, :]), line.shape)
    col_lse[...] = joined(parts[:, 1, :])

    def body(rows):
        dual = row_dual[rows, :]
        total = jnp.zeros_like(dual)
        for t in range(TILES):
            value = jnp.exp(raised[rows, tile(t)] + dual + line[0:1, tile(t)])
            joint[rows, tile(t)] = value
            total += value
        acc[rows, :] = total

    row_chunks(32, body)
    copy_out(sums, along(acc[...]))


def col_step_kernel(joint, parts, sums, scale):
    scale[...] = down(1.0 / gathered(parts))
    for t in range(TILES):
        total = jnp.sum(joint[:, tile(t)] * scale[...], axis=0, keepdims=True)
        for k in range(16):
            sums[k, :, tile(t)] = total


def row_step_kernel(joint, parts, sums, line, acc):
    line[...] = jnp.broadcast_to(0.5 / gathered(parts), line.shape)

    def body(rows):
        total = joint[rows, tile(0)] * line[0:1, tile(0)]
        for t in range(1, TILES):
            total += joint[rows, tile(t)] * line[0:1, tile(t)]
        acc[rows, :] = total

    row_chunks(32, body)
    copy_out(sums, along(acc[...]))


def last_col_kernel(joint, parts, scale, sums):
    scale[...] = down(1.0 / gathered(parts))
    for t in range(TILES):
        total = jnp.sum(joint[:, tile(t)] * scale[...], axis=0, keepdims=True)
        for k in range(16):
            sums[k, :, tile(t)] = total


def last_row_kernel(
    joint, plain, row_lse, col_lse, row_scale, parts, col_scale, sums, line, acc0, acc1, acc2
):
    factor = 0.5 / gathered(parts)
    col_scale[...] = factor
    line[...] = jnp.broadcast_to(factor, line.shape)

    def body(rows):
        lse = row_lse[rows, :]
        sum0 = jnp.zeros_like(lse)
        sum1 = jnp.zeros_like(lse)
        sum2 = jnp.zeros_like(lse)
        for t in range(TILES):
            logit = plain[rows, tile(t)]
            value = joint[rows, tile(t)] * line[0:1, tile(t)]
            sum0 += value
            sum1 += value * (lse - logit)
            sum2 += value * (col_lse[0:1, tile(t)] - logit)
        acc0[rows, :] = sum0
        acc1[rows, :] = sum1
        acc2[rows, :] = sum2 * row_scale[rows, :]

    row_chunks(32, body)
    col_terms = jnp.sum(jnp.sum(acc2[...], axis=0, keepdims=True), axis=1, keepdims=True)
    terms = jnp.broadcast_to(col_terms, (1, ROWS))
    copy_out(sums, jnp.concatenate([along(acc0[...]), along(acc1[...]), terms, terms]))


def chunk_pairs(place, slope, clips_t, i):
    y, z = place[0], place[1]

    def columns(k):
        block = ((y + AWAY[i]) % SIDE) * SIDE + (z + AWAY[k]) % SIDE
        return slope[:, pl.ds(pl.multiple_of(block * LANES, LANES), LANES)]

    for k in (0, 2):
        two = jnp.concatenate([columns(k), columns(k + 1)], axis=1)
        product = jnp.dot(clips_t[...], two, preferred_element_type=F32)
        yield k, product[:, 0:LANES]
        yield k + 1, product[:, LANES:]


def slope_kernel(
    place, joint, plain, row_lse, col_lse, row_scale, col_scale, clips_t, parts, *refs
):
    slope, own_share, *to_y = refs[:4]
    both, line = refs[4:]
    total = gathered(parts)
    norm = 1.0 / total[0:1]
    row_terms = jnp.sum(total[1:2] * norm, axis=1, keepdims=True)
    share = jnp.broadcast_to(row_terms + total[2:3, 0:1], (1, LANES)) / 16384.0
    own_share[...] = share
    both[...] = row_scale[...] + down(norm)
    line[...] = jnp.broadcast_to(col_scale[...], line.shape)

    def body(rows):
        scale = both[rows, :]
        lse = row_lse[rows, :]
        for t in range(TILES):
            value = plain[rows, tile(t)]
            soft = jnp.exp(value - lse) + 0.5 * jnp.exp(value - col_lse[0:1, tile(t)])
            target = joint[rows, tile(t)] * line[0:1, tile(t)] * scale
            slope[rows, tile(t)] = (soft - target).astype(BF16)

    row_chunks(32, body)
    for i in (1, 2):
        for k, product in chunk_pairs(place, slope, clips_t, i):
            narrow(product, share, to_y[i - 1], k * PACKED)

def far_kernel(place, slope, clips_t, share, own_z, *to_z):
    for k, product in chunk_pairs(place, slope, clips_t, 3):
        if k == 0:
            own_z[...] = product
        else:
            narrow(product, share[...], to_z[k - 1], 0)


SHARE = ROWS // 8


def near_kernel(place, slope, clips_t, *own_y):
    for k, value in chunk_pairs(place, slope, clips_t, 0):
        own_y[k][...] = value


def clip_kernel(place, slope, captions, kept, sent, product):
    product[...] = lax.dot_general(
        slope[...], captions[...], (((1,), (1,)), ((), ())), preferred_element_type=F32
    )
    x, core = place[2] // 2, place[2] % 2
    near = x + 1 - 2 * (x % 2)

    def rows_for(core):
        return [
            product[pl.ds(pl.multiple_of((chip * 2 + core) * SHARE, SHARE), SHARE), :]
            for chip in (x, 3 - x, near, 3 - near)
        ]

    kept[...] = jnp.concatenate(rows_for(core))
    narrow(jnp.concatenate(rows_for(1 - core)), ZERO, sent, 0)


def halve_kernel(own, came, kept, sent):
    value = own[...] + widen(came[...])[0]
    half = value.shape[0] // 2
    kept[...] = value[0:half]
    narrow(value[half:], ZERO, sent, 0)


def add_kernel(own, came, out):
    out[...] = own[...] + widen(came[...])[0]


def total(own, own_share, parts):
    value, share = own[...], own_share[...]
    for part in parts:
        more, came = widen(part[...])
        value += more
        share += came
    return value, share


def pass_on_kernel(own, own_share, *refs):
    parts, out = refs[:-1], refs[-1]
    value, share = total(own, own_share, parts)
    narrow(value, share, out, 0)


def keep_kernel(own, own_share, *refs):
    parts, (value_out, share_out) = refs[:-2], refs[-2:]
    value_out[...], share_out[...] = total(own, own_share, parts)


def final_kernel(own_share, kept, *refs):
    parts, (caption_grad, loss) = refs[0:4], refs[4:]
    value, loss[...] = total(kept, own_share, parts)
    caption_grad[...] = jnp.transpose(value)


def body(clips, captions, caption_owner):
    row = lax.axis_index("row").astype(jnp.int32)
    col = lax.axis_index("col").astype(jnp.int32)
    place = jnp.stack([row // SIDE, row % SIDE, col, col])
    owner = (caption_owner - row * ROWS).reshape(1, COLS)
    area = ROWS * COLS

    captions_t = captions.T
    far = row_shift(captions_t, 2, 0)
    from_z = along_z([captions_t] * SIDE)
    beside = swap(clips.T, 2)
    from_z[0], two = call(
        local_kernel,
        [captions_t, clips.T, beside],
        [shape((CAPTION_PIECE, COLS), BF16), shape((2 * CLIP_PIECE, ROWS), BF16)],
        "local",
        flops=2**33,
        moved=2**20,
    )
    far, from_z = lax.optimization_barrier((far, from_z))
    joined = join(from_z)
    clips_here = pair(two, swap(two, 6))
    clips_rows, clips_t = call(
        clips_kernel,
        [place, clips_here, swap(clips_here, 1)],
        [pltpu.VMEM((ROWS, WIDTH), BF16), pltpu.VMEM((WIDTH, ROWS), BF16)],
        "clips",
        smem=1,
        moved=2**21,
    )
    from_y = along_y([joined] * 3)
    from_z = along_z([far] * SIDE)

    captions_full, plain, raised, stats = call(
        logits_kernel,
        [place, owner, clips_rows, *from_z, *from_y],
        [
            pltpu.VMEM((WIDTH, COLS), BF16),
            pltpu.VMEM((ROWS, COLS), F32),
            pltpu.VMEM((ROWS, COLS), F32),
            shape((8, 2, ROWS)),
        ],
        "logits",
        [pltpu.VMEM((ROWS, LANES), F32)] * 3,
        smem=1,
        limit=12,
        flops=2 * area * WIDTH,
        moved=20 * 2**20,
        exps=2 * area,
    )
    parts = col_all(stats)
    row_dual, row_lse, stats = call(
        first_cols_kernel,
        [raised, plain, parts],
        [pltpu.VMEM((ROWS, LANES), F32), pltpu.VMEM((ROWS, LANES), F32), shape((16, 2, COLS))],
        "first_cols",
        flops=6 * area,
        moved=4 * area,
        exps=area,
    )
    parts = row_all(stats)
    joint, col_lse, sums = call(
        joint_kernel,
        [raised, row_dual, parts],
        [pltpu.VMEM((ROWS, COLS), F32), shape((1, COLS)), shape((8, 1, ROWS))],
        "joint",
        [pltpu.VMEM((8, COLS), F32), pltpu.VMEM((ROWS, LANES), F32)],
        flops=6 * area,
        moved=8 * area,
        exps=area,
    )
    parts = col_all(sums)
    (sums,) = call(
        col_step_kernel,
        [joint, parts],
        [shape((16, 1, COLS))],
        "col_step",
        [pltpu.VMEM((ROWS, LANES), F32)],
        flops=2 * area,
        moved=4 * area,
    )
    (sums,) = call(
        row_step_kernel,
        [joint, row_all(sums)],
        [shape((8, 1, ROWS))],
        "row_step",
        [pltpu.VMEM((8, COLS), F32), pltpu.VMEM((ROWS, LANES), F32)],
        flops=2 * area,
        moved=4 * area,
    )
    row_scale, sums = call(
        last_col_kernel,
        [joint, col_all(sums)],
        [pltpu.VMEM((ROWS, LANES), F32), shape((16, 1, COLS))],
        "last_col",
        flops=2 * area,
        moved=4 * area,
    )
    col_scale, sums = call(
        last_row_kernel,
        [joint, plain, row_lse, col_lse, row_scale, row_all(sums)],
        [shape((1, COLS)), shape((8, 4, ROWS))],
        "last_row",
        [pltpu.VMEM((8, COLS), F32)] + [pltpu.VMEM((ROWS, LANES), F32)] * 3,
        flops=8 * area,
        moved=8 * area,
    )

    def packed(chunks):
        return shape((chunks * PACKED, LANES), jnp.int16)

    slope, share, *to_y = call(
        slope_kernel,
        [place, joint, plain, row_lse, col_lse, row_scale, col_scale, clips_t, col_all(sums)],
        [pltpu.VMEM((ROWS, COLS), BF16), shape((1, LANES))] + [packed(SIDE)] * 2,
        "slope",
        [pltpu.VMEM((ROWS, LANES), F32), pltpu.VMEM((8, COLS), F32)],
        smem=1,
        flops=area * WIDTH,
        moved=12 * area,
        exps=2 * area,
    )
    from_y = along_y([None, *to_y])[1:]
    own_z, *to_z = call(
        far_kernel,
        [place, slope, clips_t, share],
        [shape((WIDTH, LANES))] + [packed(1)] * 3,
        "far",
        smem=1,
        flops=area * WIDTH // 2,
        moved=8 * area,
    )
    two_away = row_shift(to_z[2], 0, 2)
    from_z = [row_shift(to_z[0], 0, 1), row_shift(to_z[1], 0, 3), two_away]
    own_z, slope = lax.optimization_barrier((own_z, slope))
    clip_own, sent = call(
        clip_kernel,
        [place, slope, captions_full],
        [shape((4 * SHARE, WIDTH)), shape((4 * SHARE + EXTRA, WIDTH), jnp.int16)],
        "clip_share",
        [pltpu.VMEM((ROWS, WIDTH), F32)],
        smem=1,
        flops=2 * area * WIDTH,
        moved=8 * area,
    )
    came = swap(sent, 1)
    own_y0, own_y1, own_y2, own_y3 = call(
        near_kernel,
        [place, slope, clips_t],
        [shape((WIDTH, LANES))] * 4,
        "near",
        smem=1,
        flops=area * WIDTH // 2,
        moved=4 * area,
    )
    came, own_y0 = lax.optimization_barrier((came, own_y0))
    from_y, came_z = lax.optimization_barrier((from_y, from_z))
    from_z, all_sent = [], []
    for k, own in ((1, own_y1), (2, own_y2), (3, own_y3)):
        chunk = pl.BlockSpec((PACKED, LANES), lambda step, k=k: (k, 0))
        (sent_z,) = call(
            pass_on_kernel,
            [own, share, *from_y],
            [packed(1)],
            "pass_on_z",
            moved=2**21,
            specs=[VM, VM, chunk, chunk],
            grid=(1,),
        )
        all_sent.append(sent_z)
        from_z.append(row_shift(sent_z, 0, AWAY[k]))
    (sent_on,) = call(pass_on_kernel, [own_z, share, *came_z], [packed(1)], "pass_on_y", moved=2**21)
    from_y2 = row_shift(sent_on, 2, 0)
    chunk = pl.BlockSpec((PACKED, LANES), lambda step: (0, 0))
    kept, share = call(
        keep_kernel,
        [own_y0, share, *from_y],
        [shape((WIDTH, LANES)), shape((1, LANES))],
        "keep",
        moved=2**21,
        specs=[VM, VM, chunk, chunk],
        grid=(1,),
    )
    for rows, bits in ((2 * SHARE, 2), (SHARE, 6)):
        clip_own, sent = call(
            halve_kernel,
            [clip_own, came],
            [shape((rows, WIDTH)), shape((rows + EXTRA, WIDTH), jnp.int16)],
            "halve",
            moved=2**21,
        )
        came = swap(sent, bits)
    (clip_grad,) = call(add_kernel, [clip_own, came], [shape((SHARE, WIDTH))], "clip_add")
    clip_grad, kept = lax.optimization_barrier((clip_grad, kept))
    caption_grad, loss = call(
        final_kernel,
        [share, kept, from_y2, *from_z],
        [shape((LANES, WIDTH)), shape((1, LANES))],
        "final",
        flops=area,
        moved=4 * area,
    )
    return loss[0, 0], clip_grad, caption_grad


def solution(mesh):
    in_specs = (P("row", "col"), P("col", "row"), P("col"))
    out_specs = (P(), P(("row", "col"), None), P(("col", "row"), None))
    return jax.shard_map(body, mesh=mesh, in_specs=in_specs, out_specs=out_specs, check_vma=False)
```

```python
import math

import jax
import jax.numpy as jnp
from jax import lax
from jax.experimental import pallas as pl
from jax.experimental.pallas import tpu as pltpu
from jax.sharding import PartitionSpec as P

BOOST = 4.0
HALF_LOG = math.log(0.5)
WIDTH = 768
ROWS = 512
COLS = 2048
LANES = 128
TILES = COLS // LANES
SIDE = 4
CLIP_PIECE = 96
CAPTION_PIECE = 48
EXTRA = 16
PACKED = WIDTH + EXTRA
AWAY = (0, 1, 3, 2)
F32 = jnp.float32
BF16 = jnp.bfloat16

VM = pl.BlockSpec(memory_space=pltpu.VMEM)
SM = pl.BlockSpec(memory_space=pltpu.SMEM)


def call(
    kernel, args, outs, name, scratch=(), smem=0, limit=8, flops=0, moved=0, exps=0, specs=None, grid=()
):
    return pl.pallas_call(
        kernel,
        grid=grid,
        out_shape=outs,
        in_specs=specs or [SM] * smem + [VM] * (len(args) - smem),
        out_specs=[VM] * len(outs),
        scratch_shapes=list(scratch),
        compiler_params=pltpu.CompilerParams(vmem_limit_bytes=limit * 2**20),
        cost_estimate=pl.CostEstimate(flops=flops, bytes_accessed=moved, transcendentals=exps),
        name=name,
    )(*args)


def shape(dims, kind=F32):
    return jax.ShapeDtypeStruct(dims, kind)


def row_shift(value, step_y, step_z):
    pairs = [
        (y * SIDE + z, ((y + step_y) % SIDE) * SIDE + (z + step_z) % SIDE)
        for y in range(SIDE)
        for z in range(SIDE)
    ]
    return lax.ppermute(value, "row", pairs)


def col_shift(value, step_x, flip):
    pairs = [
        (x * 2 + k, ((x + step_x) % SIDE) * 2 + (k ^ flip)) for x in range(SIDE) for k in range(2)
    ]
    return lax.ppermute(value, "col", pairs)


AWAY = (0, 1, 3, 2)


def col_all(copies):
    return lax.all_to_all(copies, "col", 0, 0, tiled=True)


def row_all(copies):
    return lax.all_to_all(copies, "row", 0, 0, tiled=True)


def swap(value, bits):
    return lax.ppermute(value, "col", [(c, c ^ bits) for c in range(8)])


def along_z(values):
    return [values[0]] + [row_shift(v, 0, d) for v, d in zip(values[1:], AWAY[1:])]


def along_y(values):
    return [values[0]] + [row_shift(v, d, 0) for v, d in zip(values[1:], AWAY[1:])]


def down(line):
    return jnp.transpose(jnp.broadcast_to(line, (LANES, line.shape[1])))


def along(block):
    return jnp.sum(jnp.transpose(block), axis=0, keepdims=True)


def copy_out(sums, value):
    for k in range(sums.shape[0]):
        sums[k] = value


def integers(packed):
    return packed.astype(jnp.int32).astype(F32)


def scale_of(steps):
    return jnp.exp2(steps * (1 / 64)) * (1 / 32000)


def steps_of(peak):
    return jnp.ceil(jnp.log2(jnp.maximum(peak, 1e-30)) * 64.0)


def halfwords(numbers):
    return jnp.round(numbers).astype(jnp.int32).astype(jnp.int16)


def widen(packed):
    rows = packed.shape[0] - EXTRA
    tail = integers(packed[rows:])
    share = (tail[2:3] + tail[3:4] * 2.0**-14) * scale_of(tail[1:2])
    return integers(packed[0:rows]) * scale_of(tail[0:1]), share


ZERO = 0.0


def narrow(value, share, out, start):
    rows, lanes = value.shape
    steps = steps_of(jnp.max(jnp.abs(value), axis=0, keepdims=True))
    out[start : start + rows] = halfwords(value * (1.0 / scale_of(steps)))
    share = share + jnp.zeros((1, lanes), F32)
    share_steps = steps_of(jnp.abs(share))
    scaled = share * (1.0 / scale_of(share_steps))
    high = jnp.round(scaled)
    low = (scaled - high) * 2.0**14
    row = lax.broadcasted_iota(jnp.int32, (EXTRA, lanes), 0)
    tail = jnp.where(
        row == 0, steps, jnp.where(row == 1, share_steps, jnp.where(row == 2, high, low))
    )
    out[start + rows : start + rows + EXTRA] = halfwords(tail)


def gathered(parts):
    total = parts[0]
    for k in range(1, parts.shape[0]):
        total += parts[k]
    return total


def joined(lses):
    peak = jnp.max(lses, axis=0, keepdims=True)
    return peak + jnp.log(jnp.sum(jnp.exp(lses - peak), axis=0, keepdims=True))


def tile(t):
    return slice(t * LANES, (t + 1) * LANES)


def row_chunks(step, body):
    def run(i, carry):
        body(pl.ds(pl.multiple_of(i * step, step), step))
        return carry

    lax.fori_loop(0, ROWS // step, run, 0, unroll=4)


def local_kernel(captions, clips, beside, captions_out, clips_out):
    captions_out[...] = captions[...]
    clips_out[0:CLIP_PIECE] = clips[...]
    clips_out[CLIP_PIECE:] = beside[...]


def join_kernel(*refs):
    parts, out = refs[:-1], refs[-1]
    for k, part in enumerate(parts):
        out[:, k * COLS : (k + 1) * COLS] = part[...]


def join(parts):
    dims = (CAPTION_PIECE, len(parts) * COLS)
    return call(join_kernel, parts, [shape(dims, BF16)], "join", moved=2**21)[0]


def pair_kernel(first, second, out):
    rows = first.shape[0]
    out[0:rows] = first[...]
    out[rows:] = second[...]


def pair(first, second):
    dims = (2 * first.shape[0], ROWS)
    return call(pair_kernel, [first, second], [shape(dims, BF16)], "pair", moved=2**20)[0]


def clips_kernel(place, here, there, clips, clips_t):
    x, core = place[2] // 2, place[2] % 2
    near = x + 1 - 2 * (x % 2)
    for k, part in enumerate((here, there)):
        for i, chip in enumerate((x, near, 3 - x, 3 - near)):
            rows = pl.ds(pl.multiple_of((2 * chip + (core + k) % 2) * CLIP_PIECE, 16), CLIP_PIECE)
            clips_t[rows, :] = part[i * CLIP_PIECE : (i + 1) * CLIP_PIECE]
    clips[...] = jnp.transpose(clips_t[...])


def logits_kernel(place, owner, clips, *refs):
    from_z, from_y, outs, (acc0, acc1, peaks) = refs[:4], refs[4:7], refs[7:11], refs[11:]
    captions, plain, raised, stats = outs
    y, z = place[0], place[1]

    def put(i, k, piece):
        block = ((y - AWAY[i] + SIDE) % SIDE) * SIDE + (z - AWAY[k] + SIDE) % SIDE
        rows = pl.ds(pl.multiple_of(block * CAPTION_PIECE, 16), CAPTION_PIECE)
        captions[rows, :] = piece

    for k in range(SIDE):
        for i in range(3):
            put(i, k, from_y[i][:, k * COLS : (k + 1) * COLS])
        put(3, k, from_z[k][...])
    scale = 1.0 / math.sqrt(WIDTH)
    for n in range(4):
        at = slice(n * 512, (n + 1) * 512)
        product = jnp.dot(clips[...], captions[:, at], preferred_element_type=F32) * scale
        plain[:, at] = product
        ids = lax.broadcasted_iota(jnp.int32, (ROWS, 512), 0)
        raised[:, at] = product + BOOST * (ids == owner[:, at]).astype(F32)

    def peak_body(rows):
        best = plain[rows, tile(0)]
        for t in range(1, TILES):
            best = jnp.maximum(best, plain[rows, tile(t)])
        best = jnp.broadcast_to(jnp.max(best, axis=1, keepdims=True), best.shape) + BOOST
        peaks[rows, :] = best
        sum0 = jnp.zeros_like(best)
        sum1 = jnp.zeros_like(best)
        for t in range(TILES):
            value = plain[rows, tile(t)]
            term = jnp.exp(value - best)
            sum0 += term
            sum1 += jnp.where(raised[rows, tile(t)] > value, term * math.exp(BOOST), term)
        acc0[rows, :] = sum0
        acc1[rows, :] = sum1

    row_chunks(32, peak_body)
    best = jnp.max(jnp.transpose(peaks[...]), axis=0, keepdims=True)
    copy_out(stats, best + jnp.log(jnp.concatenate([along(acc1[...]), along(acc0[...])])))


def first_cols_kernel(raised, plain, parts, row_dual, row_lse, stats):
    row_dual[...] = down(-joined(parts[:, 0, :]))
    row_lse[...] = down(joined(parts[:, 1, :]))
    for t in range(TILES):
        block = raised[:, tile(t)] + row_dual[...]
        best = jnp.max(block, axis=0, keepdims=True)
        total = jnp.sum(jnp.exp(block - best), axis=0, keepdims=True)
        block = plain[:, tile(t)]
        best_plain = jnp.max(block, axis=0, keepdims=True)
        total_plain = jnp.sum(jnp.exp(block - best_plain), axis=0, keepdims=True)
        line = jnp.concatenate([best + jnp.log(total), best_plain + jnp.log(total_plain)])
        for k in range(16):
            stats[k, :, tile(t)] = line


def joint_kernel(raised, row_dual, parts, joint, col_lse, sums, line, acc):
    line[...] = jnp.broadcast_to(HALF_LOG - joined(parts[:, 0, :]), line.shape)
    col_lse[...] = joined(parts[:, 1, :])

    def body(rows):
        dual = row_dual[rows, :]
        total = jnp.zeros_like(dual)
        for t in range(TILES):
            value = jnp.exp(raised[rows, tile(t)] + dual + line[0:1, tile(t)])
            joint[rows, tile(t)] = value
            total += value
        acc[rows, :] = total

    row_chunks(32, body)
    copy_out(sums, along(acc[...]))


def col_step_kernel(joint, parts, sums, scale):
    scale[...] = down(1.0 / gathered(parts))
    for t in range(TILES):
        total = jnp.sum(joint[:, tile(t)] * scale[...], axis=0, keepdims=True)
        for k in range(16):
            sums[k, :, tile(t)] = total


def row_step_kernel(joint, parts, sums, line, acc):
    line[...] = jnp.broadcast_to(0.5 / gathered(parts), line.shape)

    def body(rows):
        total = joint[rows, tile(0)] * line[0:1, tile(0)]
        for t in range(1, TILES):
            total += joint[rows, tile(t)] * line[0:1, tile(t)]
        acc[rows, :] = total

    row_chunks(32, body)
    copy_out(sums, along(acc[...]))


def last_col_kernel(joint, parts, scale, sums):
    scale[...] = down(1.0 / gathered(parts))
    for t in range(TILES):
        total = jnp.sum(joint[:, tile(t)] * scale[...], axis=0, keepdims=True)
        for k in range(16):
            sums[k, :, tile(t)] = total


def last_row_kernel(
    joint, plain, row_lse, col_lse, row_scale, parts, col_scale, sums, line, acc0, acc1, acc2
):
    factor = 0.5 / gathered(parts)
    col_scale[...] = factor
    line[...] = jnp.broadcast_to(factor, line.shape)

    def body(rows):
        lse = row_lse[rows, :]
        sum0 = jnp.zeros_like(lse)
        sum1 = jnp.zeros_like(lse)
        sum2 = jnp.zeros_like(lse)
        for t in range(TILES):
            logit = plain[rows, tile(t)]
            value = joint[rows, tile(t)] * line[0:1, tile(t)]
            sum0 += value
            sum1 += value * (lse - logit)
            sum2 += value * (col_lse[0:1, tile(t)] - logit)
        acc0[rows, :] = sum0
        acc1[rows, :] = sum1
        acc2[rows, :] = sum2 * row_scale[rows, :]

    row_chunks(32, body)
    col_terms = jnp.sum(jnp.sum(acc2[...], axis=0, keepdims=True), axis=1, keepdims=True)
    terms = jnp.broadcast_to(col_terms, (1, ROWS))
    copy_out(sums, jnp.concatenate([along(acc0[...]), along(acc1[...]), terms, terms]))


def chunk_pairs(place, slope, clips_t, i):
    y, z = place[0], place[1]

    def columns(k):
        block = ((y + AWAY[i]) % SIDE) * SIDE + (z + AWAY[k]) % SIDE
        return slope[:, pl.ds(pl.multiple_of(block * LANES, LANES), LANES)]

    for k in (0, 2):
        two = jnp.concatenate([columns(k), columns(k + 1)], axis=1)
        product = jnp.dot(clips_t[...], two, preferred_element_type=F32)
        yield k, product[:, 0:LANES]
        yield k + 1, product[:, LANES:]


def slope_kernel(
    place, joint, plain, row_lse, col_lse, row_scale, col_scale, clips_t, parts, *refs
):
    slope, own_share, *to_y = refs[:4]
    both, line = refs[4:]
    total = gathered(parts)
    norm = 1.0 / total[0:1]
    row_terms = jnp.sum(total[1:2] * norm, axis=1, keepdims=True)
    share = jnp.broadcast_to(row_terms + total[2:3, 0:1], (1, LANES)) / 16384.0
    own_share[...] = share
    both[...] = row_scale[...] + down(norm)
    line[...] = jnp.broadcast_to(col_scale[...], line.shape)

    def body(rows):
        scale = both[rows, :]
        lse = row_lse[rows, :]
        for t in range(TILES):
            value = plain[rows, tile(t)]
            soft = jnp.exp(value - lse) + 0.5 * jnp.exp(value - col_lse[0:1, tile(t)])
            target = joint[rows, tile(t)] * line[0:1, tile(t)] * scale
            slope[rows, tile(t)] = (soft - target).astype(BF16)

    row_chunks(32, body)
    for i in (1, 2):
        for k, product in chunk_pairs(place, slope, clips_t, i):
            narrow(product, share, to_y[i - 1], k * PACKED)

def far_kernel(place, slope, clips_t, share, own_z, *to_z):
    for k, product in chunk_pairs(place, slope, clips_t, 3):
        if k == 0:
            own_z[...] = product
        else:
            narrow(product, share[...], to_z[k - 1], 0)


SHARE = ROWS // 8


def near_kernel(place, slope, clips_t, *own_y):
    for k, value in chunk_pairs(place, slope, clips_t, 0):
        own_y[k][...] = value


def clip_kernel(place, slope, captions, kept, sent, product):
    product[...] = lax.dot_general(
        slope[...], captions[...], (((1,), (1,)), ((), ())), preferred_element_type=F32
    )
    x, core = place[2] // 2, place[2] % 2
    near = x + 1 - 2 * (x % 2)

    def rows_for(core):
        return [
            product[pl.ds(pl.multiple_of((chip * 2 + core) * SHARE, SHARE), SHARE), :]
            for chip in (x, 3 - x, near, 3 - near)
        ]

    kept[...] = jnp.concatenate(rows_for(core))
    narrow(jnp.concatenate(rows_for(1 - core)), ZERO, sent, 0)


def halve_kernel(own, came, kept, sent):
    value = own[...] + widen(came[...])[0]
    half = value.shape[0] // 2
    kept[...] = value[0:half]
    narrow(value[half:], ZERO, sent, 0)


def add_kernel(own, came, out):
    out[...] = own[...] + widen(came[...])[0]


def total(own, own_share, parts):
    value, share = own[...], own_share[...]
    for part in parts:
        more, came = widen(part[...])
        value += more
        share += came
    return value, share


def pass_on_kernel(own, own_share, *refs):
    parts, out = refs[:-1], refs[-1]
    value, share = total(own, own_share, parts)
    narrow(value, share, out, 0)


def keep_kernel(own, own_share, *refs):
    parts, (value_out, share_out) = refs[:-2], refs[-2:]
    value_out[...], share_out[...] = total(own, own_share, parts)


def final_kernel(own_share, kept, *refs):
    parts, (caption_grad, loss) = refs[0:4], refs[4:]
    value, loss[...] = total(kept, own_share, parts)
    caption_grad[...] = jnp.transpose(value)


def body(clips, captions, caption_owner):
    row = lax.axis_index("row").astype(jnp.int32)
    col = lax.axis_index("col").astype(jnp.int32)
    place = jnp.stack([row // SIDE, row % SIDE, col, col])
    owner = (caption_owner - row * ROWS).reshape(1, COLS)
    area = ROWS * COLS

    captions_t = captions.T
    far = row_shift(captions_t, 2, 0)
    from_z = along_z([captions_t] * SIDE)
    beside = swap(clips.T, 2)
    from_z[0], two = call(
        local_kernel,
        [captions_t, clips.T, beside],
        [shape((CAPTION_PIECE, COLS), BF16), shape((2 * CLIP_PIECE, ROWS), BF16)],
        "local",
        flops=2**33,
        moved=2**20,
    )
    far, from_z = lax.optimization_barrier((far, from_z))
    joined = join(from_z)
    clips_here = pair(two, swap(two, 6))
    clips_rows, clips_t = call(
        clips_kernel,
        [place, clips_here, swap(clips_here, 1)],
        [pltpu.VMEM((ROWS, WIDTH), BF16), pltpu.VMEM((WIDTH, ROWS), BF16)],
        "clips",
        smem=1,
        moved=2**21,
    )
    from_y = along_y([joined] * 3)
    from_z = along_z([far] * SIDE)

    captions_full, plain, raised, stats = call(
        logits_kernel,
        [place, owner, clips_rows, *from_z, *from_y],
        [
            pltpu.VMEM((WIDTH, COLS), BF16),
            pltpu.VMEM((ROWS, COLS), F32),
            pltpu.VMEM((ROWS, COLS), F32),
            shape((8, 2, ROWS)),
        ],
        "logits",
        [pltpu.VMEM((ROWS, LANES), F32)] * 3,
        smem=1,
        limit=12,
        flops=2 * area * WIDTH,
        moved=20 * 2**20,
        exps=2 * area,
    )
    parts = col_all(stats)
    row_dual, row_lse, stats = call(
        first_cols_kernel,
        [raised, plain, parts],
        [pltpu.VMEM((ROWS, LANES), F32), pltpu.VMEM((ROWS, LANES), F32), shape((16, 2, COLS))],
        "first_cols",
        flops=6 * area,
        moved=4 * area,
        exps=area,
    )
    parts = row_all(stats)
    joint, col_lse, sums = call(
        joint_kernel,
        [raised, row_dual, parts],
        [pltpu.VMEM((ROWS, COLS), F32), shape((1, COLS)), shape((8, 1, ROWS))],
        "joint",
        [pltpu.VMEM((8, COLS), F32), pltpu.VMEM((ROWS, LANES), F32)],
        flops=6 * area,
        moved=8 * area,
        exps=area,
    )
    parts = col_all(sums)
    (sums,) = call(
        col_step_kernel,
        [joint, parts],
        [shape((16, 1, COLS))],
        "col_step",
        [pltpu.VMEM((ROWS, LANES), F32)],
        flops=2 * area,
        moved=4 * area,
    )
    (sums,) = call(
        row_step_kernel,
        [joint, row_all(sums)],
        [shape((8, 1, ROWS))],
        "row_step",
        [pltpu.VMEM((8, COLS), F32), pltpu.VMEM((ROWS, LANES), F32)],
        flops=2 * area,
        moved=4 * area,
    )
    row_scale, sums = call(
        last_col_kernel,
        [joint, col_all(sums)],
        [pltpu.VMEM((ROWS, LANES), F32), shape((16, 1, COLS))],
        "last_col",
        flops=2 * area,
        moved=4 * area,
    )
    col_scale, sums = call(
        last_row_kernel,
        [joint, plain, row_lse, col_lse, row_scale, row_all(sums)],
        [shape((1, COLS)), shape((8, 4, ROWS))],
        "last_row",
        [pltpu.VMEM((8, COLS), F32)] + [pltpu.VMEM((ROWS, LANES), F32)] * 3,
        flops=8 * area,
        moved=8 * area,
    )

    def packed(chunks):
        return shape((chunks * PACKED, LANES), jnp.int16)

    slope, share, *to_y = call(
        slope_kernel,
        [place, joint, plain, row_lse, col_lse, row_scale, col_scale, clips_t, col_all(sums)],
        [pltpu.VMEM((ROWS, COLS), BF16), shape((1, LANES))] + [packed(SIDE)] * 2,
        "slope",
        [pltpu.VMEM((ROWS, LANES), F32), pltpu.VMEM((8, COLS), F32)],
        smem=1,
        flops=area * WIDTH,
        moved=12 * area,
        exps=2 * area,
    )
    from_y = along_y([None, *to_y])[1:]
    own_z, *to_z = call(
        far_kernel,
        [place, slope, clips_t, share],
        [shape((WIDTH, LANES))] + [packed(1)] * 3,
        "far",
        smem=1,
        flops=area * WIDTH // 2,
        moved=8 * area,
    )
    two_away = row_shift(to_z[2], 0, 2)
    from_z = [row_shift(to_z[0], 0, 1), row_shift(to_z[1], 0, 3), two_away]
    own_z, slope = lax.optimization_barrier((own_z, slope))
    clip_own, sent = call(
        clip_kernel,
        [place, slope, captions_full],
        [shape((4 * SHARE, WIDTH)), shape((4 * SHARE + EXTRA, WIDTH), jnp.int16)],
        "clip_share",
        [pltpu.VMEM((ROWS, WIDTH), F32)],
        smem=1,
        flops=2 * area * WIDTH,
        moved=8 * area,
    )
    came = swap(sent, 1)
    own_y0, own_y1, own_y2, own_y3 = call(
        near_kernel,
        [place, slope, clips_t],
        [shape((WIDTH, LANES))] * 4,
        "near",
        smem=1,
        flops=area * WIDTH // 2,
        moved=4 * area,
    )
    came, own_y0 = lax.optimization_barrier((came, own_y0))
    from_y, came_z = lax.optimization_barrier((from_y, from_z))
    from_z, all_sent = [], []
    for k, own in ((1, own_y1), (2, own_y2), (3, own_y3)):
        chunk = pl.BlockSpec((PACKED, LANES), lambda step, k=k: (k, 0))
        (sent_z,) = call(
            pass_on_kernel,
            [own, share, *from_y],
            [packed(1)],
            "pass_on_z",
            moved=2**21,
            specs=[VM, VM, chunk, chunk],
            grid=(1,),
        )
        all_sent.append(sent_z)
        from_z.append(row_shift(sent_z, 0, AWAY[k]))
    (sent_on,) = call(pass_on_kernel, [own_z, share, *came_z], [packed(1)], "pass_on_y", moved=2**21)
    from_y2 = row_shift(sent_on, 2, 0)
    chunk = pl.BlockSpec((PACKED, LANES), lambda step: (0, 0))
    kept, share = call(
        keep_kernel,
        [own_y0, share, *from_y],
        [shape((WIDTH, LANES)), shape((1, LANES))],
        "keep",
        moved=2**21,
        specs=[VM, VM, chunk, chunk],
        grid=(1,),
    )
    for rows, bits in ((2 * SHARE, 2), (SHARE, 6)):
        clip_own, sent = call(
            halve_kernel,
            [clip_own, came],
            [shape((rows, WIDTH)), shape((rows + EXTRA, WIDTH), jnp.int16)],
            "halve",
            moved=2**21,
        )
        came = swap(sent, bits)
    (clip_grad,) = call(add_kernel, [clip_own, came], [shape((SHARE, WIDTH))], "clip_add")
    clip_grad, kept = lax.optimization_barrier((clip_grad, kept))
    caption_grad, loss = call(
        final_kernel,
        [share, kept, from_y2, *from_z],
        [shape((LANES, WIDTH)), shape((1, LANES))],
        "final",
        flops=area,
        moved=4 * area,
    )
    return loss[0, 0], clip_grad, caption_grad


def solution(mesh):
    in_specs = (P("row", "col"), P("col", "row"), P("col"))
    out_specs = (P(), P(("row", "col"), None), P(("col", "row"), None))
    return jax.shard_map(body, mesh=mesh, in_specs=in_specs, out_specs=out_specs, check_vma=False)
```

```python
import math

import jax
import jax.numpy as jnp
from jax import lax
from jax.experimental import pallas as pl
from jax.experimental.pallas import tpu as pltpu
from jax.sharding import PartitionSpec as P

BOOST = 4.0
HALF_LOG = math.log(0.5)
WIDTH = 768
ROWS = 512
COLS = 2048
LANES = 128
TILES = COLS // LANES
SIDE = 4
CLIP_PIECE = 96
CAPTION_PIECE = 48
EXTRA = 16
PACKED = WIDTH + EXTRA
AWAY = (0, 1, 3, 2)
F32 = jnp.float32
BF16 = jnp.bfloat16

VM = pl.BlockSpec(memory_space=pltpu.VMEM)
SM = pl.BlockSpec(memory_space=pltpu.SMEM)


def call(
    kernel, args, outs, name, scratch=(), smem=0, limit=8, flops=0, moved=0, exps=0, specs=None, grid=()
):
    return pl.pallas_call(
        kernel,
        grid=grid,
        out_shape=outs,
        in_specs=specs or [SM] * smem + [VM] * (len(args) - smem),
        out_specs=[VM] * len(outs),
        scratch_shapes=list(scratch),
        compiler_params=pltpu.CompilerParams(vmem_limit_bytes=limit * 2**20),
        cost_estimate=pl.CostEstimate(flops=flops, bytes_accessed=moved, transcendentals=exps),
        name=name,
    )(*args)


def shape(dims, kind=F32):
    return jax.ShapeDtypeStruct(dims, kind)


def row_shift(value, step_y, step_z):
    pairs = [
        (y * SIDE + z, ((y + step_y) % SIDE) * SIDE + (z + step_z) % SIDE)
        for y in range(SIDE)
        for z in range(SIDE)
    ]
    return lax.ppermute(value, "row", pairs)


def col_shift(value, step_x, flip):
    pairs = [
        (x * 2 + k, ((x + step_x) % SIDE) * 2 + (k ^ flip)) for x in range(SIDE) for k in range(2)
    ]
    return lax.ppermute(value, "col", pairs)


AWAY = (0, 1, 3, 2)


def col_all(copies):
    return lax.all_to_all(copies, "col", 0, 0, tiled=True)


def row_all(copies):
    return lax.all_to_all(copies, "row", 0, 0, tiled=True)


def swap(value, bits):
    return lax.ppermute(value, "col", [(c, c ^ bits) for c in range(8)])


def along_z(values):
    return [values[0]] + [row_shift(v, 0, d) for v, d in zip(values[1:], AWAY[1:])]


def along_y(values):
    return [values[0]] + [row_shift(v, d, 0) for v, d in zip(values[1:], AWAY[1:])]


def down(line):
    return jnp.transpose(jnp.broadcast_to(line, (LANES, line.shape[1])))


def along(block):
    return jnp.sum(jnp.transpose(block), axis=0, keepdims=True)


def copy_out(sums, value):
    for k in range(sums.shape[0]):
        sums[k] = value


def integers(packed):
    return packed.astype(jnp.int32).astype(F32)


def scale_of(steps):
    return jnp.exp2(steps * (1 / 64)) * (1 / 32000)


def steps_of(peak):
    return jnp.ceil(jnp.log2(jnp.maximum(peak, 1e-30)) * 64.0)


def halfwords(numbers):
    return jnp.round(numbers).astype(jnp.int32).astype(jnp.int16)


def widen(packed):
    rows = packed.shape[0] - EXTRA
    tail = integers(packed[rows:])
    share = (tail[2:3] + tail[3:4] * 2.0**-14) * scale_of(tail[1:2])
    return integers(packed[0:rows]) * scale_of(tail[0:1]), share


ZERO = 0.0


def narrow(value, share, out, start):
    rows, lanes = value.shape
    steps = steps_of(jnp.max(jnp.abs(value), axis=0, keepdims=True))
    out[start : start + rows] = halfwords(value * (1.0 / scale_of(steps)))
    share = share + jnp.zeros((1, lanes), F32)
    share_steps = steps_of(jnp.abs(share))
    scaled = share * (1.0 / scale_of(share_steps))
    high = jnp.round(scaled)
    low = (scaled - high) * 2.0**14
    row = lax.broadcasted_iota(jnp.int32, (EXTRA, lanes), 0)
    tail = jnp.where(
        row == 0, steps, jnp.where(row == 1, share_steps, jnp.where(row == 2, high, low))
    )
    out[start + rows : start + rows + EXTRA] = halfwords(tail)


def gathered(parts):
    total = parts[0]
    for k in range(1, parts.shape[0]):
        total += parts[k]
    return total


def joined(lses):
    peak = jnp.max(lses, axis=0, keepdims=True)
    return peak + jnp.log(jnp.sum(jnp.exp(lses - peak), axis=0, keepdims=True))


def tile(t):
    return slice(t * LANES, (t + 1) * LANES)


def row_chunks(step, body):
    def run(i, carry):
        body(pl.ds(pl.multiple_of(i * step, step), step))
        return carry

    lax.fori_loop(0, ROWS // step, run, 0, unroll=8)


def local_kernel(captions, clips, beside, captions_out, clips_out):
    captions_out[...] = captions[...]
    clips_out[0:CLIP_PIECE] = clips[...]
    clips_out[CLIP_PIECE:] = beside[...]


def join_kernel(*refs):
    parts, out = refs[:-1], refs[-1]
    for k, part in enumerate(parts):
        out[:, k * COLS : (k + 1) * COLS] = part[...]


def join(parts):
    dims = (CAPTION_PIECE, len(parts) * COLS)
    return call(join_kernel, parts, [shape(dims, BF16)], "join", moved=2**21)[0]


def pair_kernel(first, second, out):
    rows = first.shape[0]
    out[0:rows] = first[...]
    out[rows:] = second[...]


def pair(first, second):
    dims = (2 * first.shape[0], ROWS)
    return call(pair_kernel, [first, second], [shape(dims, BF16)], "pair", moved=2**20)[0]


def clips_kernel(place, here, there, clips, clips_t):
    x, core = place[2] // 2, place[2] % 2
    near = x + 1 - 2 * (x % 2)
    for k, part in enumerate((here, there)):
        for i, chip in enumerate((x, near, 3 - x, 3 - near)):
            rows = pl.ds(pl.multiple_of((2 * chip + (core + k) % 2) * CLIP_PIECE, 16), CLIP_PIECE)
            clips_t[rows, :] = part[i * CLIP_PIECE : (i + 1) * CLIP_PIECE]
    clips[...] = jnp.transpose(clips_t[...])


def logits_kernel(place, owner, clips, *refs):
    from_z, from_y, outs, (acc0, acc1, peaks) = refs[:4], refs[4:7], refs[7:11], refs[11:]
    captions, plain, raised, stats = outs
    y, z = place[0], place[1]

    def put(i, k, piece):
        block = ((y - AWAY[i] + SIDE) % SIDE) * SIDE + (z - AWAY[k] + SIDE) % SIDE
        rows = pl.ds(pl.multiple_of(block * CAPTION_PIECE, 16), CAPTION_PIECE)
        captions[rows, :] = piece

    for k in range(SIDE):
        for i in range(3):
            put(i, k, from_y[i][:, k * COLS : (k + 1) * COLS])
        put(3, k, from_z[k][...])
    scale = 1.0 / math.sqrt(WIDTH)
    for n in range(4):
        at = slice(n * 512, (n + 1) * 512)
        product = jnp.dot(clips[...], captions[:, at], preferred_element_type=F32) * scale
        plain[:, at] = product
        ids = lax.broadcasted_iota(jnp.int32, (ROWS, 512), 0)
        raised[:, at] = product + BOOST * (ids == owner[:, at]).astype(F32)

    def peak_body(rows):
        best = plain[rows, tile(0)]
        for t in range(1, TILES):
            best = jnp.maximum(best, plain[rows, tile(t)])
        best = jnp.broadcast_to(jnp.max(best, axis=1, keepdims=True), best.shape) + BOOST
        peaks[rows, :] = best
        sum0 = jnp.zeros_like(best)
        sum1 = jnp.zeros_like(best)
        for t in range(TILES):
            value = plain[rows, tile(t)]
            term = jnp.exp(value - best)
            sum0 += term
            sum1 += jnp.where(raised[rows, tile(t)] > value, term * math.exp(BOOST), term)
        acc0[rows, :] = sum0
        acc1[rows, :] = sum1

    row_chunks(32, peak_body)
    best = jnp.max(jnp.transpose(peaks[...]), axis=0, keepdims=True)
    copy_out(stats, best + jnp.log(jnp.concatenate([along(acc1[...]), along(acc0[...])])))


def first_cols_kernel(raised, plain, parts, row_dual, row_lse, stats):
    row_dual[...] = down(-joined(parts[:, 0, :]))
    row_lse[...] = down(joined(parts[:, 1, :]))
    for t in range(TILES):
        block = raised[:, tile(t)] + row_dual[...]
        best = jnp.max(block, axis=0, keepdims=True)
        total = jnp.sum(jnp.exp(block - best), axis=0, keepdims=True)
        block = plain[:, tile(t)]
        best_plain = jnp.max(block, axis=0, keepdims=True)
        total_plain = jnp.sum(jnp.exp(block - best_plain), axis=0, keepdims=True)
        line = jnp.concatenate([best + jnp.log(total), best_plain + jnp.log(total_plain)])
        for k in range(16):
            stats[k, :, tile(t)] = line


def joint_kernel(raised, row_dual, parts, joint, col_lse, sums, line, acc):
    line[...] = jnp.broadcast_to(HALF_LOG - joined(parts[:, 0, :]), line.shape)
    col_lse[...] = joined(parts[:, 1, :])

    def body(rows):
        dual = row_dual[rows, :]
        total = jnp.zeros_like(dual)
        for t in range(TILES):
            value = jnp.exp(raised[rows, tile(t)] + dual + line[0:1, tile(t)])
            joint[rows, tile(t)] = value
            total += value
        acc[rows, :] = total

    row_chunks(32, body)
    copy_out(sums, along(acc[...]))


def col_step_kernel(joint, parts, sums, scale):
    scale[...] = down(1.0 / gathered(parts))
    for t in range(TILES):
        total = jnp.sum(joint[:, tile(t)] * scale[...], axis=0, keepdims=True)
        for k in range(16):
            sums[k, :, tile(t)] = total


def row_step_kernel(joint, parts, sums, line, acc):
    line[...] = jnp.broadcast_to(0.5 / gathered(parts), line.shape)

    def body(rows):
        total = joint[rows, tile(0)] * line[0:1, tile(0)]
        for t in range(1, TILES):
            total += joint[rows, tile(t)] * line[0:1, tile(t)]
        acc[rows, :] = total

    row_chunks(32, body)
    copy_out(sums, along(acc[...]))


def last_col_kernel(joint, parts, scale, sums):
    scale[...] = down(1.0 / gathered(parts))
    for t in range(TILES):
        total = jnp.sum(joint[:, tile(t)] * scale[...], axis=0, keepdims=True)
        for k in range(16):
            sums[k, :, tile(t)] = total


def last_row_kernel(
    joint, plain, row_lse, col_lse, row_scale, parts, col_scale, sums, line, acc0, acc1, acc2
):
    factor = 0.5 / gathered(parts)
    col_scale[...] = factor
    line[...] = jnp.broadcast_to(factor, line.shape)

    def body(rows):
        lse = row_lse[rows, :]
        sum0 = jnp.zeros_like(lse)
        sum1 = jnp.zeros_like(lse)
        sum2 = jnp.zeros_like(lse)
        for t in range(TILES):
            logit = plain[rows, tile(t)]
            value = joint[rows, tile(t)] * line[0:1, tile(t)]
            sum0 += value
            sum1 += value * (lse - logit)
            sum2 += value * (col_lse[0:1, tile(t)] - logit)
        acc0[rows, :] = sum0
        acc1[rows, :] = sum1
        acc2[rows, :] = sum2 * row_scale[rows, :]

    row_chunks(32, body)
    col_terms = jnp.sum(jnp.sum(acc2[...], axis=0, keepdims=True), axis=1, keepdims=True)
    terms = jnp.broadcast_to(col_terms, (1, ROWS))
    copy_out(sums, jnp.concatenate([along(acc0[...]), along(acc1[...]), terms, terms]))


def chunk_pairs(place, slope, clips_t, i):
    y, z = place[0], place[1]

    def columns(k):
        block = ((y + AWAY[i]) % SIDE) * SIDE + (z + AWAY[k]) % SIDE
        return slope[:, pl.ds(pl.multiple_of(block * LANES, LANES), LANES)]

    for k in (0, 2):
        two = jnp.concatenate([columns(k), columns(k + 1)], axis=1)
        product = jnp.dot(clips_t[...], two, preferred_element_type=F32)
        yield k, product[:, 0:LANES]
        yield k + 1, product[:, LANES:]


def slope_kernel(
    place, joint, plain, row_lse, col_lse, row_scale, col_scale, clips_t, parts, *refs
):
    slope, own_share, *to_y = refs[:4]
    both, line = refs[4:]
    total = gathered(parts)
    norm = 1.0 / total[0:1]
    row_terms = jnp.sum(total[1:2] * norm, axis=1, keepdims=True)
    share = jnp.broadcast_to(row_terms + total[2:3, 0:1], (1, LANES)) / 16384.0
    own_share[...] = share
    both[...] = row_scale[...] + down(norm)
    line[...] = jnp.broadcast_to(col_scale[...], line.shape)

    def body(rows):
        scale = both[rows, :]
        lse = row_lse[rows, :]
        for t in range(TILES):
            value = plain[rows, tile(t)]
            soft = jnp.exp(value - lse) + 0.5 * jnp.exp(value - col_lse[0:1, tile(t)])
            target = joint[rows, tile(t)] * line[0:1, tile(t)] * scale
            slope[rows, tile(t)] = (soft - target).astype(BF16)

    row_chunks(32, body)
    for i in (1, 2):
        for k, product in chunk_pairs(place, slope, clips_t, i):
            narrow(product, share, to_y[i - 1], k * PACKED)

def far_kernel(place, slope, clips_t, share, own_z, *to_z):
    for k, product in chunk_pairs(place, slope, clips_t, 3):
        if k == 0:
            own_z[...] = product
        else:
            narrow(product, share[...], to_z[k - 1], 0)


SHARE = ROWS // 8


def near_kernel(place, slope, clips_t, *own_y):
    for k, value in chunk_pairs(place, slope, clips_t, 0):
        own_y[k][...] = value


def clip_kernel(place, slope, captions, kept, sent, product):
    product[...] = lax.dot_general(
        slope[...], captions[...], (((1,), (1,)), ((), ())), preferred_element_type=F32
    )
    x, core = place[2] // 2, place[2] % 2
    near = x + 1 - 2 * (x % 2)

    def rows_for(core):
        return [
            product[pl.ds(pl.multiple_of((chip * 2 + core) * SHARE, SHARE), SHARE), :]
            for chip in (x, 3 - x, near, 3 - near)
        ]

    kept[...] = jnp.concatenate(rows_for(core))
    narrow(jnp.concatenate(rows_for(1 - core)), ZERO, sent, 0)


def halve_kernel(own, came, kept, sent):
    value = own[...] + widen(came[...])[0]
    half = value.shape[0] // 2
    kept[...] = value[0:half]
    narrow(value[half:], ZERO, sent, 0)


def add_kernel(own, came, out):
    out[...] = own[...] + widen(came[...])[0]


def total(own, own_share, parts):
    value, share = own[...], own_share[...]
    for part in parts:
        more, came = widen(part[...])
        value += more
        share += came
    return value, share


def pass_on_kernel(own, own_share, *refs):
    parts, out = refs[:-1], refs[-1]
    value, share = total(own, own_share, parts)
    narrow(value, share, out, 0)


def keep_kernel(own, own_share, *refs):
    parts, (value_out, share_out) = refs[:-2], refs[-2:]
    value_out[...], share_out[...] = total(own, own_share, parts)


def final_kernel(own_share, kept, *refs):
    parts, (caption_grad, loss) = refs[0:4], refs[4:]
    value, loss[...] = total(kept, own_share, parts)
    caption_grad[...] = jnp.transpose(value)


def body(clips, captions, caption_owner):
    row = lax.axis_index("row").astype(jnp.int32)
    col = lax.axis_index("col").astype(jnp.int32)
    place = jnp.stack([row // SIDE, row % SIDE, col, col])
    owner = (caption_owner - row * ROWS).reshape(1, COLS)
    area = ROWS * COLS

    captions_t = captions.T
    far = row_shift(captions_t, 2, 0)
    from_z = along_z([captions_t] * SIDE)
    beside = swap(clips.T, 2)
    from_z[0], two = call(
        local_kernel,
        [captions_t, clips.T, beside],
        [shape((CAPTION_PIECE, COLS), BF16), shape((2 * CLIP_PIECE, ROWS), BF16)],
        "local",
        flops=2**33,
        moved=2**20,
    )
    far, from_z = lax.optimization_barrier((far, from_z))
    joined = join(from_z)
    clips_here = pair(two, swap(two, 6))
    clips_rows, clips_t = call(
        clips_kernel,
        [place, clips_here, swap(clips_here, 1)],
        [pltpu.VMEM((ROWS, WIDTH), BF16), pltpu.VMEM((WIDTH, ROWS), BF16)],
        "clips",
        smem=1,
        moved=2**21,
    )
    from_y = along_y([joined] * 3)
    from_z = along_z([far] * SIDE)

    captions_full, plain, raised, stats = call(
        logits_kernel,
        [place, owner, clips_rows, *from_z, *from_y],
        [
            pltpu.VMEM((WIDTH, COLS), BF16),
            pltpu.VMEM((ROWS, COLS), F32),
            pltpu.VMEM((ROWS, COLS), F32),
            shape((8, 2, ROWS)),
        ],
        "logits",
        [pltpu.VMEM((ROWS, LANES), F32)] * 3,
        smem=1,
        limit=12,
        flops=2 * area * WIDTH,
        moved=20 * 2**20,
        exps=2 * area,
    )
    parts = col_all(stats)
    row_dual, row_lse, stats = call(
        first_cols_kernel,
        [raised, plain, parts],
        [pltpu.VMEM((ROWS, LANES), F32), pltpu.VMEM((ROWS, LANES), F32), shape((16, 2, COLS))],
        "first_cols",
        flops=6 * area,
        moved=4 * area,
        exps=area,
    )
    parts = row_all(stats)
    joint, col_lse, sums = call(
        joint_kernel,
        [raised, row_dual, parts],
        [pltpu.VMEM((ROWS, COLS), F32), shape((1, COLS)), shape((8, 1, ROWS))],
        "joint",
        [pltpu.VMEM((8, COLS), F32), pltpu.VMEM((ROWS, LANES), F32)],
        flops=6 * area,
        moved=8 * area,
        exps=area,
    )
    parts = col_all(sums)
    (sums,) = call(
        col_step_kernel,
        [joint, parts],
        [shape((16, 1, COLS))],
        "col_step",
        [pltpu.VMEM((ROWS, LANES), F32)],
        flops=2 * area,
        moved=4 * area,
    )
    (sums,) = call(
        row_step_kernel,
        [joint, row_all(sums)],
        [shape((8, 1, ROWS))],
        "row_step",
        [pltpu.VMEM((8, COLS), F32), pltpu.VMEM((ROWS, LANES), F32)],
        flops=2 * area,
        moved=4 * area,
    )
    row_scale, sums = call(
        last_col_kernel,
        [joint, col_all(sums)],
        [pltpu.VMEM((ROWS, LANES), F32), shape((16, 1, COLS))],
        "last_col",
        flops=2 * area,
        moved=4 * area,
    )
    col_scale, sums = call(
        last_row_kernel,
        [joint, plain, row_lse, col_lse, row_scale, row_all(sums)],
        [shape((1, COLS)), shape((8, 4, ROWS))],
        "last_row",
        [pltpu.VMEM((8, COLS), F32)] + [pltpu.VMEM((ROWS, LANES), F32)] * 3,
        flops=8 * area,
        moved=8 * area,
    )

    def packed(chunks):
        return shape((chunks * PACKED, LANES), jnp.int16)

    slope, share, *to_y = call(
        slope_kernel,
        [place, joint, plain, row_lse, col_lse, row_scale, col_scale, clips_t, col_all(sums)],
        [pltpu.VMEM((ROWS, COLS), BF16), shape((1, LANES))] + [packed(SIDE)] * 2,
        "slope",
        [pltpu.VMEM((ROWS, LANES), F32), pltpu.VMEM((8, COLS), F32)],
        smem=1,
        flops=area * WIDTH,
        moved=12 * area,
        exps=2 * area,
    )
    from_y = along_y([None, *to_y])[1:]
    own_z, *to_z = call(
        far_kernel,
        [place, slope, clips_t, share],
        [shape((WIDTH, LANES))] + [packed(1)] * 3,
        "far",
        smem=1,
        flops=area * WIDTH // 2,
        moved=8 * area,
    )
    two_away = row_shift(to_z[2], 0, 2)
    from_z = [row_shift(to_z[0], 0, 1), row_shift(to_z[1], 0, 3), two_away]
    own_z, slope = lax.optimization_barrier((own_z, slope))
    clip_own, sent = call(
        clip_kernel,
        [place, slope, captions_full],
        [shape((4 * SHARE, WIDTH)), shape((4 * SHARE + EXTRA, WIDTH), jnp.int16)],
        "clip_share",
        [pltpu.VMEM((ROWS, WIDTH), F32)],
        smem=1,
        flops=2 * area * WIDTH,
        moved=8 * area,
    )
    came = swap(sent, 1)
    own_y0, own_y1, own_y2, own_y3 = call(
        near_kernel,
        [place, slope, clips_t],
        [shape((WIDTH, LANES))] * 4,
        "near",
        smem=1,
        flops=area * WIDTH // 2,
        moved=4 * area,
    )
    came, own_y0 = lax.optimization_barrier((came, own_y0))
    from_y, came_z = lax.optimization_barrier((from_y, from_z))
    from_z, all_sent = [], []
    for k, own in ((1, own_y1), (2, own_y2), (3, own_y3)):
        chunk = pl.BlockSpec((PACKED, LANES), lambda step, k=k: (k, 0))
        (sent_z,) = call(
            pass_on_kernel,
            [own, share, *from_y],
            [packed(1)],
            "pass_on_z",
            moved=2**21,
            specs=[VM, VM, chunk, chunk],
            grid=(1,),
        )
        all_sent.append(sent_z)
        from_z.append(row_shift(sent_z, 0, AWAY[k]))
    (sent_on,) = call(pass_on_kernel, [own_z, share, *came_z], [packed(1)], "pass_on_y", moved=2**21)
    from_y2 = row_shift(sent_on, 2, 0)
    chunk = pl.BlockSpec((PACKED, LANES), lambda step: (0, 0))
    kept, share = call(
        keep_kernel,
        [own_y0, share, *from_y],
        [shape((WIDTH, LANES)), shape((1, LANES))],
        "keep",
        moved=2**21,
        specs=[VM, VM, chunk, chunk],
        grid=(1,),
    )
    for rows, bits in ((2 * SHARE, 2), (SHARE, 6)):
        clip_own, sent = call(
            halve_kernel,
            [clip_own, came],
            [shape((rows, WIDTH)), shape((rows + EXTRA, WIDTH), jnp.int16)],
            "halve",
            moved=2**21,
        )
        came = swap(sent, bits)
    (clip_grad,) = call(add_kernel, [clip_own, came], [shape((SHARE, WIDTH))], "clip_add")
    clip_grad, kept = lax.optimization_barrier((clip_grad, kept))
    caption_grad, loss = call(
        final_kernel,
        [share, kept, from_y2, *from_z],
        [shape((LANES, WIDTH)), shape((1, LANES))],
        "final",
        flops=area,
        moved=4 * area,
    )
    return loss[0, 0], clip_grad, caption_grad


def solution(mesh):
    in_specs = (P("row", "col"), P("col", "row"), P("col"))
    out_specs = (P(), P(("row", "col"), None), P(("col", "row"), None))
    return jax.shard_map(body, mesh=mesh, in_specs=in_specs, out_specs=out_specs, check_vma=False)
```
